128 devices in a mesh: section: 2 (over z_hi), lat: 8 (over y, core), lon: 8 (over z_lo, x).
Axes of the slice: x: 4, y: 4, z: 4 (z_hi: 2, z_lo: 2; z = z_hi * 2 + z_lo), core: 2. Of those that a mesh axis runs over, the one named last changes fastest.
Arguments:
- latent: bfloat16 [2, 4, 96, 192, 512], P('section', None, 'lat', 'lon'), may hold values from -11 to 11
- skip: bfloat16 [2, 4, 96, 192, 512], P('section', None, 'lat', 'lon'), may hold values from -6 to 6
- lat_valid: int32 [96], replicated, may hold values from 0 to 1, as said below
- level_group: int32 [13], replicated, may hold values from 0 to 3, as said below
- w_qkv: bfloat16 [512, 1536], replicated, may hold values from -0.25 to 0.25
- w_attn_out: bfloat16 [512, 512], replicated, may hold values from -0.25 to 0.25
- gain_attn: float32 [512], replicated, may hold values from 0.1 to 1.9
- w_up: bfloat16 [512, 2048], replicated, may hold values from -0.25 to 0.25
- w_down: bfloat16 [2048, 512], replicated, may hold values from -0.125 to 0.125
- gain_mlp: float32 [512], replicated, may hold values from 0.1 to 1.9
- dec_query: bfloat16 [13, 1024], replicated, may hold values from -6 to 6
- w_dec_k: bfloat16 [1024, 1024], replicated, may hold values from -0.1875 to 0.1875
- w_dec_v: bfloat16 [1024, 1024], replicated, may hold values from -0.1875 to 0.1875
- w_head: bfloat16 [1024, 500], replicated, may hold values from -0.1875 to 0.1875
- w_patch: bfloat16 [500, 512], replicated, may hold values from -0.25 to 0.25
- enc_embed: bfloat16 [13, 512], replicated, may hold values from -6 to 6
- lat_query: bfloat16 [4, 512], replicated, may hold values from -6 to 6
- w_enc_k: bfloat16 [512, 512], replicated, may hold values from -0.25 to 0.25
- w_enc_v: bfloat16 [512, 512], replicated, may hold values from -0.25 to 0.25
- w_enc_out: bfloat16 [512, 512], replicated, may hold values from -0.25 to 0.25
Outputs:
- fields: bfloat16 [2, 13, 96, 96000], P('section', None, 'lat', 'lon')
- next_latent: bfloat16 [2, 4, 96, 192, 512], P('section', None, 'lat', 'lon')
The draws below stay inside these ranges and needn't reach their ends.
Inputs may be any that keep to these rules, and one draw needn't show every extreme that they name: `lat_valid`: 1 on every row except the final 1 to 6 rows, which are 0. `level_group`: every latent level is named by at least one pressure level.
All inputs are finite; a program needn't handle non-finite values.
Results may differ from the reference program's by a relative error of at most 0.025.
Values may be sent and summed in bfloat16 or wider, within the bound.
A program may use at most 128 MiB of HBM per device.

```python
import jax
import jax.numpy as jnp
from jax import lax

D = 512
LEVELS = 13
LATENT = 4
HEAD_DIM = 64
WIN_LEV = 2
WIN_LAT = 6
WIN_LON = 12
FFN = 2048
PIX = 500
MICRO = 2
NLAT = 96
NLON = 192


def draw_latent(key, part):
    key = jax.random.fold_in(key, 11)
    key_base = jax.random.fold_in(key, 0)
    full_shape = (MICRO, LATENT, NLAT, NLON, D)
    base_draw = jax.random.normal(key_base, full_shape, jnp.float32)
    return jnp.clip(base_draw, -6.0, 6.0).astype(jnp.bfloat16)


def draw_lat_valid(key, part):
    key = jax.random.fold_in(key, 23)
    padding = jax.random.randint(key, (), 1, 7)
    rows_here = jnp.arange(NLAT, dtype=jnp.int32)
    return (rows_here < NLAT - padding).astype(jnp.int32)


def draw_level_group(key, part):
    key = jax.random.fold_in(key, 37)
    key_perm, key_rest = jax.random.split(key)
    order_perm = jax.random.permutation(key_perm, LEVELS)
    extra_groups = jax.random.randint(key_rest, (LEVELS,), 0, LATENT)
    positions = jnp.arange(LEVELS, dtype=jnp.int32)
    base_draw = jnp.where(positions < LATENT, positions, extra_groups)
    inverse_perm = jnp.argsort(order_perm)
    return base_draw[inverse_perm].astype(jnp.int32)


def steps_of(key, dims, shards, smallest, top_value):
    level = 1.0
    for dim, shards_of in shards:
        steps = jax.random.uniform(jax.random.fold_in(jax.random.fold_in(key, 6), dim), (shards_of,), jnp.float32, smallest / len(shards), top_value / len(shards))
        level = level * jnp.repeat(jnp.exp(steps), dims[dim] // shards_of).reshape((-1,) + (1,) * (len(dims) - 1 - dim))
    return level


def gaussian(rng, extent, scale, most, cuts=(), kind=jnp.bfloat16):
    entries = jax.random.normal(rng, extent, jnp.float32) * scale
    if len(cuts) > 0:
        entries = steps_of(rng, extent, cuts, -0.22, 0.18) * entries
    return jnp.clip(entries, min=-most, max=most).astype(kind)


def setup_inputs(seed: int = 0) -> dict:
    seeds = jax.random.split(jax.random.key(seed), 21)
    return {
        "latent": draw_latent(jax.random.fold_in(seeds[20], 71), 0),
        "skip": gaussian(seeds[1], (MICRO, LATENT, NLAT, NLON, D), 1.0, 6.0, ((0, 2), (2, 8), (3, 8))),
        "lat_valid": draw_lat_valid(jax.random.fold_in(seeds[20], 71), 0),
        "level_group": draw_level_group(jax.random.fold_in(seeds[20], 71), 0),
        "w_qkv": gaussian(seeds[4], (D, 3 * D), D ** -0.5, 0.25),
        "w_attn_out": gaussian(seeds[5], (D, D), D ** -0.5, 0.25),
        "gain_attn": jnp.clip(1.0 + 0.18 * jax.random.normal(seeds[6], (D,), jnp.float32), 0.1, 1.9),
        "w_up": gaussian(seeds[7], (D, FFN), D ** -0.5, 0.25),
        "w_down": gaussian(seeds[8], (FFN, D), FFN ** -0.5, 0.125),
        "gain_mlp": jnp.clip(1.0 + 0.18 * jax.random.normal(seeds[9], (D,), jnp.float32), 0.1, 1.9),
        "dec_query": gaussian(seeds[10], (LEVELS, 2 * D), 1.0, 6.0),
        "w_dec_k": gaussian(seeds[11], (2 * D, 2 * D), (2 * D) ** -0.5, 0.1875),
        "w_dec_v": gaussian(seeds[12], (2 * D, 2 * D), (2 * D) ** -0.5, 0.1875),
        "w_head": gaussian(seeds[13], (2 * D, PIX), (2 * D) ** -0.5, 0.1875),
        "w_patch": gaussian(seeds[14], (PIX, D), PIX ** -0.5, 0.25),
        "enc_embed": gaussian(seeds[15], (LEVELS, D), 1.0, 6.0),
        "lat_query": gaussian(seeds[16], (LATENT, D), 1.0, 6.0),
        "w_enc_k": gaussian(seeds[17], (D, D), D ** -0.5, 0.25),
        "w_enc_v": gaussian(seeds[18], (D, D), D ** -0.5, 0.25),
        "w_enc_out": gaussian(seeds[19], (D, D), D ** -0.5, 0.25),
    }


SCALE = 0.125
MASKED = -1e+30

def layer_norm(value, gain):
    mean_value = lax.optimization_barrier(jnp.mean(value, axis=-1, keepdims=True))
    centred = value - mean_value
    variance = lax.optimization_barrier(jnp.mean(centred * centred, axis=-1, keepdims=True))
    return centred * lax.rsqrt(variance + 1e-05) * gain

def windows(blocks):
    level_count, row_count, col_count = blocks.shape[:3]
    trailing = blocks.shape[3:]
    blocks = blocks.reshape((level_count // WIN_LEV, WIN_LEV, row_count // WIN_LAT, WIN_LAT, col_count // WIN_LON, WIN_LON) + trailing)
    axes_order = (0, 2, 4, 1, 3, 5) + tuple(range(6, 6 + len(trailing)))
    return blocks.transpose(axes_order).reshape((-1, WIN_LEV * WIN_LAT * WIN_LON) + trailing)

def unwindows(blocks, level_count, row_count, col_count):
    trailing = blocks.shape[2:]
    blocks = blocks.reshape((level_count // WIN_LEV, row_count // WIN_LAT, col_count // WIN_LON, WIN_LEV, WIN_LAT, WIN_LON) + trailing)
    axes_order = (0, 3, 1, 4, 2, 5) + tuple(range(6, 6 + len(trailing)))
    return blocks.transpose(axes_order).reshape((level_count, row_count, col_count) + trailing)

def attend(tokens, lat_index, row_valid, w_qkv, w_attn_out, gain_attn):
    level_count, row_count, col_count, features = tokens.shape
    head_count = features // HEAD_DIM
    qkv = jnp.dot(tokens.reshape(-1, features), w_qkv, preferred_element_type=jnp.float32).astype(jnp.bfloat16)
    qkv = windows(qkv.reshape(level_count, row_count, col_count, 3, head_count, HEAD_DIM))
    queries = qkv[:, :, 0]
    key_rows = qkv[:, :, 1]
    values = qkv[:, :, 2]
    shift_lev = WIN_LEV // 2
    lev_index = (jnp.arange(level_count, dtype=jnp.int32) + shift_lev) % level_count
    lev_label = (lev_index + shift_lev) // WIN_LEV
    lat_label = (lat_index + WIN_LAT // 2) // WIN_LAT
    filler = jnp.ones((level_count, row_count, col_count), jnp.int32)
    lev_win = windows(lev_label[:, None, None] * filler)
    lat_win = windows(lat_label[None, :, None] * filler)
    valid_win = windows(row_valid[None, :, None] * filler)
    window_len = lev_win.shape[1]
    same_group = (lev_win[:, :, None] == lev_win[:, None, :]) & (lat_win[:, :, None] == lat_win[:, None, :])
    allowed = same_group & ((valid_win[:, None, :] > 0) | jnp.eye(window_len, dtype=bool)[None])
    scores = jnp.einsum('wqhd,wkhd->whqk', queries.astype(jnp.float32), key_rows.astype(jnp.float32)) * SCALE
    scores = jnp.where(allowed[:, None], scores, MASKED)
    row_max = lax.optimization_barrier(jnp.max(scores, axis=-1, keepdims=True))
    exp_scores = jnp.exp(scores - row_max)
    weights = (exp_scores / lax.optimization_barrier(jnp.sum(exp_scores, axis=-1, keepdims=True))).astype(jnp.bfloat16)
    mixed_heads = jnp.einsum('whqk,wkhd->wqhd', weights.astype(jnp.float32), values.astype(jnp.float32)).astype(jnp.bfloat16)
    mixed_heads = unwindows(mixed_heads.reshape(mixed_heads.shape[0], window_len, features), level_count, row_count, col_count)
    attn_out = jnp.dot(mixed_heads.reshape(-1, features), w_attn_out, preferred_element_type=jnp.float32)
    result = tokens.reshape(-1, features).astype(jnp.float32) + layer_norm(attn_out, gain_attn)
    return result.astype(jnp.bfloat16).reshape(level_count, row_count, col_count, features)

def feed_forward(tokens, w_up, w_down, gain_mlp):
    features = tokens.shape[-1]
    flattened = tokens.reshape(-1, features)
    hidden = jax.nn.gelu(jnp.dot(flattened, w_up, preferred_element_type=jnp.float32), approximate=False).astype(jnp.bfloat16)
    projected = jnp.dot(hidden, w_down, preferred_element_type=jnp.float32)
    result = flattened.astype(jnp.float32) + layer_norm(projected, gain_mlp)
    return result.astype(jnp.bfloat16).reshape(tokens.shape)

def decode(tokens, skip_tokens, dec_query, w_dec_k, w_dec_v, w_head):
    level_count, row_count, col_count, model_width = tokens.shape
    features = 2 * model_width
    head_count = features // HEAD_DIM
    positions = row_count * col_count
    flattened = jnp.concatenate([tokens, skip_tokens], axis=-1).reshape(-1, features)
    key_rows = jnp.dot(flattened, w_dec_k, preferred_element_type=jnp.float32).astype(jnp.bfloat16).reshape(level_count, positions, head_count, HEAD_DIM)
    values = jnp.dot(flattened, w_dec_v, preferred_element_type=jnp.float32).astype(jnp.bfloat16).reshape(level_count, positions, head_count, HEAD_DIM)
    queries = dec_query.reshape(-1, head_count, HEAD_DIM)
    scores = jnp.einsum('lhd,gphd->lgph', queries.astype(jnp.float32), key_rows.astype(jnp.float32)) * SCALE
    row_max = lax.optimization_barrier(jnp.max(scores, axis=1, keepdims=True))
    exp_scores = jnp.exp(scores - row_max)
    weights = (exp_scores / lax.optimization_barrier(jnp.sum(exp_scores, axis=1, keepdims=True))).astype(jnp.bfloat16)
    mixed_heads = jnp.einsum('lgph,gphd->lphd', weights.astype(jnp.float32), values.astype(jnp.float32)).astype(jnp.bfloat16)
    fields = jnp.dot(mixed_heads.reshape(-1, features), w_head, preferred_element_type=jnp.float32).astype(jnp.bfloat16)
    return fields.reshape(queries.shape[0], row_count, col_count * w_head.shape[1])

def encode(fields, level_group, w_patch, enc_embed, lat_query, w_enc_k, w_enc_v, w_enc_out):
    level_count, row_count, flat_cols = fields.shape
    pixels, features = w_patch.shape
    col_count = flat_cols // pixels
    positions = row_count * col_count
    head_count = features // HEAD_DIM
    embedded = jnp.dot(fields.reshape(-1, pixels), w_patch, preferred_element_type=jnp.float32).reshape(level_count, positions, features)
    embedded = (embedded + enc_embed.astype(jnp.float32)[:, None, :]).astype(jnp.bfloat16).reshape(-1, features)
    key_rows = jnp.dot(embedded, w_enc_k, preferred_element_type=jnp.float32).astype(jnp.bfloat16).reshape(level_count, positions, head_count, HEAD_DIM)
    values = jnp.dot(embedded, w_enc_v, preferred_element_type=jnp.float32).astype(jnp.bfloat16).reshape(level_count, positions, head_count, HEAD_DIM)
    queries = lat_query.reshape(-1, head_count, HEAD_DIM)
    latent_count = queries.shape[0]
    scores = jnp.einsum('ghd,lphd->glph', queries.astype(jnp.float32), key_rows.astype(jnp.float32)) * SCALE
    member = level_group[None, :] == jnp.arange(latent_count, dtype=jnp.int32)[:, None]
    scores = jnp.where(member[:, :, None, None], scores, MASKED)
    row_max = lax.optimization_barrier(jnp.max(scores, axis=1, keepdims=True))
    exp_scores = jnp.exp(scores - row_max)
    weights = (exp_scores / lax.optimization_barrier(jnp.sum(exp_scores, axis=1, keepdims=True))).astype(jnp.bfloat16)
    mixed_heads = jnp.einsum('glph,lphd->gphd', weights.astype(jnp.float32), values.astype(jnp.float32)).astype(jnp.bfloat16)
    result = jnp.dot(mixed_heads.reshape(-1, features), w_enc_out, preferred_element_type=jnp.float32).astype(jnp.bfloat16)
    return result.reshape(latent_count, row_count, col_count, features)

def reference(latent, skip, lat_valid, level_group, w_qkv, w_attn_out, gain_attn, w_up, w_down, gain_mlp, dec_query, w_dec_k, w_dec_v, w_head, w_patch, enc_embed, lat_query, w_enc_k, w_enc_v, w_enc_out):
    micro_count, level_count, lat_total, lon_total, features = latent.shape
    band_count = lat_total // WIN_LAT
    rolled_rows = (jnp.arange(lat_total, dtype=jnp.int32) + WIN_LAT // 2) % lat_total
    valid_rows = lat_valid[rolled_rows]

    def one_band(band_item):
        tokens, lat_index, row_valid = band_item
        return attend(tokens, lat_index, row_valid, w_qkv, w_attn_out, gain_attn)

    def decode_band(band_item):
        tokens, skip_tokens = band_item
        return decode(feed_forward(tokens, w_up, w_down, gain_mlp), skip_tokens, dec_query, w_dec_k, w_dec_v, w_head)

    def encode_band(band_fields):
        return encode(band_fields, level_group, w_patch, enc_embed, lat_query, w_enc_k, w_enc_v, w_enc_out)
    fields_all = []
    for micro_index in range(micro_count):
        rolled = jnp.roll(latent[micro_index], (-(WIN_LEV // 2), -(WIN_LAT // 2), -(WIN_LON // 2)), axis=(0, 1, 2))
        banded = rolled.reshape(level_count, band_count, WIN_LAT, lon_total, features).transpose(1, 0, 2, 3, 4)
        attended = lax.map(one_band, (banded, rolled_rows.reshape(band_count, WIN_LAT), valid_rows.reshape(band_count, WIN_LAT)))
        attended = attended.transpose(1, 0, 2, 3, 4).reshape(level_count, lat_total, lon_total, features)
        attended = jnp.roll(attended, (WIN_LAT // 2, WIN_LON // 2), axis=(1, 2))
        banded = attended.reshape(level_count, band_count, WIN_LAT, lon_total, features).transpose(1, 0, 2, 3, 4)
        skip_rolled = jnp.roll(skip[micro_index], -(WIN_LEV // 2), axis=0)
        skip_banded = skip_rolled.reshape(level_count, band_count, WIN_LAT, lon_total, features).transpose(1, 0, 2, 3, 4)
        fields = lax.map(decode_band, (banded, skip_banded))
        fields = fields.transpose(1, 0, 2, 3).reshape(fields.shape[1], lat_total, -1)
        fields_all.append(fields)
    next_list = []
    for micro_index in range(micro_count):
        source = fields_all[micro_count - 1 - micro_index]
        banded = source.reshape(source.shape[0], band_count, WIN_LAT, source.shape[2]).transpose(1, 0, 2, 3)
        encoded = lax.map(encode_band, banded)
        encoded = encoded.transpose(1, 0, 2, 3, 4).reshape(encoded.shape[1], lat_total, lon_total, features)
        next_list.append(encoded)
    return (jnp.stack(fields_all), jnp.stack(next_list))
```

```python
import functools

import jax
import jax.numpy as jnp
import numpy as np
from jax import lax
from jax.experimental import pallas as pl
from jax.experimental.pallas import tpu as pltpu
from jax.sharding import PartitionSpec as P

F32 = jnp.float32
BF16 = jnp.bfloat16
SCALE = 0.125
MASKED = -1e30
VMEM_LIMIT = 56 * 1024 * 1024
NPOS = 144
NTOK = 4 * NPOS
NLEV = 13


def dot(a, b):
    return lax.dot_general(a, b, (((1,), (0,)), ((), ())), preferred_element_type=F32)


def dot_t(a, b):
    return lax.dot_general(a, b, (((1,), (1,)), ((), ())), preferred_element_type=F32)


def params():
    return pltpu.CompilerParams(vmem_limit_bytes=VMEM_LIMIT)


VSPEC = pl.BlockSpec(memory_space=pltpu.VMEM)
SSPEC = pl.BlockSpec(memory_space=pltpu.SMEM)


def norm(value, gain):
    mean = jnp.mean(value, axis=-1, keepdims=True)
    centred = value - mean
    variance = jnp.mean(centred * centred, axis=-1, keepdims=True)
    return centred * lax.rsqrt(variance + 1e-05) * gain


def prep_kernel(
    valid, group, dq, wdk, wp, wek, wev, lq, emb,
    wq_out, wpv_out, wps_out, csb_out, ce_out, bias_out, qb, qe,
):
    lat = lax.axis_index("lat")
    masks = []
    for axis in range(2):
        token = lax.broadcasted_iota(jnp.int32, (144, 144), axis)
        masks.append((token, (token >= 72).astype(jnp.int32)))
    lines = [((t - 72 * vv) * 10923) >> 17 for t, vv in masks]
    same_level = masks[0][1] == masks[1][1]
    same_token = masks[0][0] == masks[1][0]
    for band in range(2):
        first = [(lat * 12 + 3 + band * 6 + rr) % 96 for rr in range(6)]
        labels = [sum(jnp.where(line == rr, (first[rr] + 3) // 6, 0) for rr in range(6)) for line in lines]
        real = sum(jnp.where(lines[1] == rr, valid[first[rr]], 0) for rr in range(6))
        allow = (labels[0] == labels[1]) & ((real > 0) | same_token)
        bias_out[band] = jnp.where(allow, 0.0, MASKED)
        bias_out[2 + band] = jnp.where(allow & same_level, 0.0, MASKED)

    head16 = lax.broadcasted_iota(jnp.int32, (16, 1024), 0)
    lane16 = lax.broadcasted_iota(jnp.int32, (16, 1024), 1)
    mask16 = (lane16 >= head16 * 64) & (lane16 < head16 * 64 + 64)
    for level in range(16):
        if level < NLEV:
            row = dq[level : level + 1, :].astype(F32)
            block = jnp.where(mask16, jnp.broadcast_to(row, (16, 1024)), 0.0)
        else:
            block = jnp.zeros((16, 1024), F32)
        qb[level * 16 : level * 16 + 16, :] = block.astype(BF16)
    wq_out[...] = (dot_t(wdk[...], qb[...]) * SCALE).astype(BF16)
    head8 = lax.broadcasted_iota(jnp.int32, (8, 512), 0)
    lane8 = lax.broadcasted_iota(jnp.int32, (8, 512), 1)
    mask8 = (lane8 >= head8 * 64) & (lane8 < head8 * 64 + 64)
    qe[...] = jnp.zeros_like(qe)
    for g in range(4):
        row = lq[g : g + 1, :].astype(F32)
        qe[g * 8 : g * 8 + 8, :] = jnp.where(mask8, jnp.broadcast_to(row, (8, 512)), 0.0)
    wkq = (dot_t(wek[...], qe[...].astype(BF16)) * SCALE).astype(BF16)
    wps_out[496:512, :] = jnp.zeros((16, 128), BF16)
    wpv_out[496:512, :] = jnp.zeros((16, 512), BF16)
    wps_out[0:500, :] = dot(wp[...], wkq).astype(BF16)
    wpv_out[0:500, :] = dot(wp[...], wev[...]).astype(BF16)
    level = lax.broadcasted_iota(jnp.int32, (NLEV, 128), 0)
    lane = lax.broadcasted_iota(jnp.int32, (NLEV, 128), 1)
    mine = sum(jnp.where(level == i, group[i], 0) for i in range(NLEV))
    member = jnp.where((lane < 32) & ((lane >> 3) != mine), MASKED, 0.0)
    csb_out[0:NLEV, :] = dot(emb[...], wkq) + member
    ce_out[0:NLEV, :] = dot(emb[...], wev[...])


def prep(valid, group, dq, wdk, wp, wek, wev, lq, emb):
    sds = jax.ShapeDtypeStruct
    return pl.pallas_call(
        prep_kernel,
        out_shape=(
            sds((1024, 256), BF16),
            sds((512, 512), BF16),
            sds((512, 128), BF16),
            sds((16, 128), F32),
            sds((16, 512), F32),
            sds((4, 144, 144), F32),
        ),
        in_specs=[SSPEC] * 2 + [VSPEC] * 7,
        out_specs=(VSPEC,) * 6,
        scratch_shapes=[pltpu.VMEM((256, 1024), BF16), pltpu.VMEM((128, 512), F32)],
        compiler_params=params(),
        cost_estimate=pl.CostEstimate(
            flops=900_000_000, bytes_accessed=6_000_000, transcendentals=0
        ),
        name="fold_weights",
    )(valid, group, dq, wdk, wp, wek, wev, lq, emb)


def attend_kernel(
    lat, in_a, in_b0, in_b1, in_c, gain, perm, perm_t, wqkv_far, bias_far, wo_far,
    out, out_a, out_b0, out_b1, out_c, wqkv, bias, wo, x_s, xp_s, qkv_s, mix_s, sems,
):
    pairs = ((wqkv_far, wqkv), (bias_far, bias), (wo_far, wo))
    loads = [pltpu.make_async_copy(a, b, sems.at[i]) for i, (a, b) in enumerate(pairs)]
    for load in loads:
        load.start()
    col8 = lax.broadcasted_iota(jnp.int32, (6, 8, 512), 1)
    for half in range(2):
        for band in range(2):
            for vv in range(2):
                level = (2 * half + vv + 1) % 4
                if band == 0:
                    own = lat[level, 3:9].astype(F32)
                    halo = in_b0[level].astype(F32)
                    first = jnp.where(col8 < 6, halo, own[:, 0:8])
                    tokens = jnp.concatenate([first, own[:, 8:24]], axis=1)
                else:
                    own = jnp.concatenate([lat[level, 9:12], in_a[level]], axis=0).astype(F32)
                    halo = jnp.concatenate([in_b1[level], in_c[level]], axis=0).astype(F32)
                    last = jnp.where(col8 >= 2, halo, own[:, 16:24])
                    tokens = jnp.concatenate([own[:, 0:16], last], axis=1)
                base = ((half * 2 + band) * 2 + vv) * 144
                x_s[base : base + 144, :] = tokens.reshape(144, 512).astype(BF16)
            base = (half * 2 + band) * 288
            rows = slice(base, base + 288)
            xp_s[rows, :] = dot(perm[...], x_s[rows, :]).astype(BF16)

    loads[0].wait()
    for part in range(4):
        rows = slice(part * 288, part * 288 + 288)
        qkv_s[rows, :] = dot(xp_s[rows, :], wqkv[...]).astype(BF16)
    loads[1].wait()
    ones = jnp.ones((144, 128), BF16)
    lane = lax.broadcasted_iota(jnp.int32, (144, 128), 1)

    def window(block, win):
        base = block * 288 + win * 144
        rows = slice(base, base + 144)
        mask = bias[block]
        mask = jnp.concatenate([mask, mask], axis=0)
        for off in range(0, 512, 128):
            q = qkv_s[rows, off : off + 128].astype(F32) * (SCALE * 1.4426950408889634)
            k = qkv_s[rows, off + 512 : off + 640]
            v = jnp.concatenate([qkv_s[rows, off + 1024 : off + 1152], ones], axis=1)
            both = jnp.concatenate([jnp.where(lane < 64, q, 0.0), jnp.where(lane < 64, 0.0, q)], axis=0)
            s = dot_t(both.astype(BF16), k) + mask
            e = jnp.exp2(s - jnp.max(s, axis=-1, keepdims=True))
            r = dot(e.astype(BF16), v)
            r = r[:, 0:128] / r[:, 128:256]
            mix_s[rows, off : off + 128] = jnp.where(lane < 64, r[0:144], r[144:288]).astype(BF16)

    for block in range(4):
        for win in range(2):
            window(block, win)
    loads[2].wait()
    for half in range(2):
        for band in range(2):
            base = (half * 2 + band) * 288
            rows = slice(base, base + 288)
            back = dot(perm_t[...], mix_s[rows, :]).astype(BF16)
            o = dot(back, wo[...])
            res = x_s[rows, :].astype(F32) + norm(o, gain[...])
            res = res.reshape(2, 6, 24, 512)
            for vv in range(2):
                level = half * 2 + vv
                if band == 0:
                    out[level, 3:9] = res[vv].astype(BF16)
                    out_b0[level] = res[vv, :, 0:8].astype(BF16)
                else:
                    out[level, 9:12] = res[vv, 0:3].astype(BF16)
                    out[level, 0:3] = res[vv, 3:6].astype(BF16)
                    out_a[level] = res[vv, 3:6].astype(BF16)
                    out_b1[level] = res[vv, 0:3, 16:24].astype(BF16)
                    out_c[level] = res[vv, 3:6, 16:24].astype(BF16)


def window_order():
    order = []
    for cols in (list(range(6, 18)), list(range(18, 24)) + list(range(6))):
        order += [line * 24 + col for line in range(12) for col in cols]
    return np.eye(288, dtype=np.float32)[order]


def attend(lat, in_a, in_b0, in_b1, in_c, bias, wqkv, wo, gain):
    sds = jax.ShapeDtypeStruct
    perm = jnp.asarray(window_order(), BF16)
    return pl.pallas_call(
        attend_kernel,
        out_shape=(
            sds((4, 12, 24, 512), BF16),
            sds((4, 3, 24, 512), BF16),
            sds((4, 6, 8, 512), BF16),
            sds((4, 3, 8, 512), BF16),
            sds((4, 3, 8, 512), BF16),
        ),
        in_specs=[VSPEC] * 8 + [pl.BlockSpec(memory_space=pl.ANY)] * 3,
        out_specs=(VSPEC,) * 5,
        scratch_shapes=[
            pltpu.VMEM((512, 1536), BF16),
            pltpu.VMEM((4, 144, 144), F32),
            pltpu.VMEM((512, 512), BF16),
            pltpu.VMEM((1152, 512), BF16),
            pltpu.VMEM((1152, 512), BF16),
            pltpu.VMEM((1152, 1536), BF16),
            pltpu.VMEM((1152, 512), BF16),
            pltpu.SemaphoreType.DMA((3,)),
        ],
        compiler_params=params(),
        cost_estimate=pl.CostEstimate(
            flops=6_000_000_000, bytes_accessed=8_000_000, transcendentals=3_000_000
        ),
        name="window_attention",
    )(lat, in_a, in_b0, in_b1, in_c, gain, perm, perm.T, wqkv, bias, wo)


def set_tokens(which, ref, level):
    own = ref[level].astype(F32)
    if which == 0:
        return jnp.concatenate([own[3:9, 8:24], own[9:12, 0:16]], axis=0).reshape(NPOS, 512)
    return jnp.concatenate(
        [
            own[0:3].reshape(72, 512),
            own[3:9, 0:8].reshape(48, 512),
            own[9:12, 16:24].reshape(24, 512),
        ],
        axis=0,
    )


def rest_kernel(which, *refs):
    group, att = refs[:2]
    refs = refs[2:]
    if which == 1:
        in_a, in_b0, in_b1, in_c = refs[:4]
        refs = refs[4:]
    (gain, csb, ce) = refs[:3]
    far = refs[3:12]
    (f_out, n_out) = refs[12:14]
    near = refs[14:23]
    (j_s, x_s, h_s, v_s, w_s, big_s, m_s, s_s, ve_s, we_s, acc_s, f_s, sems, out_sems) = refs[23:]
    (wup, wdown, skip, wv, wq, whead, wps, wpv, wout) = near
    loads = [pltpu.make_async_copy(a, b, sems.at[i]) for i, (a, b) in enumerate(zip(far, near))]
    for load in loads:
        load.start()

    col8 = lax.broadcasted_iota(jnp.int32, (3, 8, 512), 1)
    for level in range(4):
        rows = slice(level * NPOS, level * NPOS + NPOS)
        if which == 0:
            tokens = set_tokens(0, att, level)
        else:
            a = in_a[level].astype(F32)
            a_last = jnp.where(col8 >= 2, in_c[level].astype(F32), a[:, 16:24])
            top = jnp.concatenate([a[:, 0:16], a_last], axis=1).reshape(72, 512)
            left = jnp.where(
                jnp.concatenate([col8, col8], axis=0) < 6,
                in_b0[level].astype(F32),
                att[level, 3:9].astype(F32)[:, 0:8],
            ).reshape(48, 512)
            right = jnp.where(
                col8 >= 2, in_b1[level].astype(F32), att[level, 9:12].astype(F32)[:, 16:24]
            ).reshape(24, 512)
            tokens = jnp.concatenate([top, left, right], axis=0)
        x_s[rows, :] = tokens.astype(BF16)

    row = lax.broadcasted_iota(jnp.int32, (448, 1024), 0)
    head = lax.broadcasted_iota(jnp.int32, (448, 1024), 1) // 64
    big_s[...] = jnp.where(row == head + 192, 1.0, 0.0).astype(BF16)

    loads[0].wait()

    def up(step, carry):
        cols = pl.ds(pl.multiple_of(step * 512, 512), 512)
        weight = wup[:, cols]
        for part in range(2):
            rows = slice(part * 288, part * 288 + 288)
            u = dot(x_s[rows, :], weight)
            h_s[rows, cols] = (0.5 * u * (1.0 + lax.erf(u * 0.7071067811865476))).astype(BF16)
        return carry

    lax.fori_loop(0, 4, up, 0, unroll=True)

    loads[1].wait()

    def down(step, carry):
        rows = pl.ds(pl.multiple_of(step * 288, 288), 288)
        d = dot(h_s[rows, :], wdown[...])
        res = x_s[rows, :].astype(F32) + norm(d, gain[...])
        j_s[rows, 0:512] = res.astype(BF16)
        return carry

    lax.fori_loop(0, 2, down, 0, unroll=True)

    loads[2].wait()
    for level in range(4):
        rows = slice(level * NPOS, level * NPOS + NPOS)
        j_s[rows, 512:1024] = set_tokens(which, skip, (level + 1) % 4).astype(BF16)
    loads[3].wait()

    def values(step, carry):
        cols = pl.ds(pl.multiple_of(step * 256, 256), 256)
        weight = wv[:, cols]
        v0 = dot(j_s[0:NPOS, :], weight)
        v_s[0:NPOS, cols] = v0
        for level in range(1, 4):
            rows = slice(level * NPOS, level * NPOS + NPOS)
            v_s[rows, cols] = dot(j_s[rows, :], weight) - v0
        return carry

    lax.fori_loop(0, 4, values, 0, unroll=True)
    loads[4].wait()
    scores = [dot(j_s[g * NPOS : g * NPOS + NPOS, :], wq[...]) for g in range(4)]
    top = jnp.maximum(jnp.maximum(scores[0], scores[1]), jnp.maximum(scores[2], scores[3]))
    exps = [jnp.exp(s - top) for s in scores]
    inv = 1.0 / (exps[0] + exps[1] + exps[2] + exps[3])
    for g in range(1, 4):
        w_s[(g - 1) * NPOS : g * NPOS, :] = (exps[g] * inv).astype(BF16)

    def mix(level, carry):
        spread = pl.ds(pl.multiple_of(192 - 16 * level, 16), 256)
        rows = pl.ds(pl.multiple_of(level * NPOS, NPOS), NPOS)
        for part in range(4):
            cols = slice(part * 256, part * 256 + 256)
            ex = dot(w_s[...], big_s[spread, cols])
            total = v_s[0:NPOS, cols]
            for g in range(1, 4):
                here = slice(g * NPOS, g * NPOS + NPOS)
                total = total + ex[(g - 1) * NPOS : g * NPOS] * v_s[here, cols]
            m_s[rows, cols] = total.astype(BF16)
        return carry

    lax.fori_loop(0, NLEV, mix, 0, unroll=True)

    for load in loads[5:]:
        load.wait()

    def save(step):
        rows = pl.ds(pl.multiple_of(step * 624, 624), 624)
        return pltpu.make_async_copy(f_s.at[rows], f_out.at[rows], out_sems.at[step])

    f_s[:, 384:512] = jnp.zeros((NLEV * NPOS, 128), BF16)

    def heads(step, carry):
        rows = pl.ds(pl.multiple_of(step * 624, 624), 624)
        f_s[rows, 0:500] = dot_t(m_s[rows, :], whead[...]).astype(BF16)
        f = f_s[rows, :]
        save(step).start()
        s_s[rows, :] = dot(f, wps[...])
        ve_s[rows, :] = dot(f, wpv[...])
        return carry

    [heads(i,0) for i in range(3)]

    def lev(ref, level):
        return ref[level * NPOS : level * NPOS + NPOS, :]

    top = None
    for level in range(NLEV):
        s = lev(s_s, level) + csb[level : level + 1, :]
        top = s if top is None else jnp.maximum(top, s)
    total = None
    for level in range(NLEV):
        e = jnp.exp(lev(s_s, level) + csb[level : level + 1, :] - top)
        s_s[level * NPOS : level * NPOS + NPOS, :] = e
        total = e if total is None else total + e
    inv = 1.0 / total
    for level in range(NLEV):
        we_s[level * NPOS : level * NPOS + NPOS, :] = (lev(s_s, level) * inv).astype(BF16)
    acc_s[...] = jnp.zeros_like(acc_s)
    erow = lax.broadcasted_iota(jnp.int32, (128, 512), 0)
    ehead = lax.broadcasted_iota(jnp.int32, (128, 512), 1) // 64
    spread = jnp.where((erow < 32) & (erow % 8 == ehead), 1.0, 0.0).astype(BF16)
    for level in range(NLEV):
        g = group[level]
        ex = dot(lev(we_s, level), spread)
        acc_s[g] += ex * (lev(ve_s, level) + ce[level : level + 1, :])
    for g in range(4):
        n_out[g] = dot(acc_s[g].astype(BF16), wout[...]).astype(BF16)
    for step in range(3):
        save(step).wait()


def rest(which, group, att, halos, skip, *weights):
    sds = jax.ShapeDtypeStruct
    (wup, wdown, gain, wv, wq, whead, wps, wpv, csb, ce, wout) = weights
    far = (wup, wdown, skip, wv, wq, whead, wps, wpv, wout)
    any_spec = pl.BlockSpec(memory_space=pl.ANY)
    return pl.pallas_call(
        functools.partial(rest_kernel, which),
        out_shape=(sds((NLEV * NPOS, 512), BF16), sds((4, NPOS, 512), BF16)),
        in_specs=[SSPEC] + [VSPEC] * (4 + len(halos)) + [any_spec] * len(far),
        out_specs=(any_spec, VSPEC),
        scratch_shapes=[pltpu.VMEM(a.shape, a.dtype) for a in far]
        + [
            pltpu.VMEM((NTOK, 1024), BF16),
            pltpu.VMEM((NTOK, 512), BF16),
            pltpu.VMEM((NTOK, 2048), BF16),
            pltpu.VMEM((NTOK, 1024), F32),
            pltpu.VMEM((3 * NPOS, 256), BF16),
            pltpu.VMEM((448, 1024), BF16),
            pltpu.VMEM((NLEV * NPOS, 1024), BF16),
            pltpu.VMEM((NLEV * NPOS, 128), F32),
            pltpu.VMEM((NLEV * NPOS, 512), F32),
            pltpu.VMEM((NLEV * NPOS, 128), BF16),
            pltpu.VMEM((4, NPOS, 512), F32),
            pltpu.VMEM((NLEV * NPOS, 512), BF16),
            pltpu.SemaphoreType.DMA((len(far),)),
            pltpu.SemaphoreType.DMA((3,)),
        ],
        compiler_params=params(),
        cost_estimate=pl.CostEstimate(
            flops=12_000_000_000, bytes_accessed=16_000_000, transcendentals=2_000_000
        ),
        name="cells_inner" if which == 0 else "cells_border",
    )(group, att, *halos, gain, csb, ce, *far)


def fields_kernel(f0, f1, out, inner, border):
    row = pl.program_id(0)

    @pl.when(row == 0)
    def _():
        for level in range(NLEV):
            block = f1[level].astype(F32)
            for lt in range(4):
                base = lt * 16 * NPOS + level * NPOS
                border[base : base + NPOS, :] = block[:, lt * 128 : lt * 128 + 128]

    for level in range(NLEV):
        block = f0[level, 0].astype(F32)
        for lt in range(4):
            base = lt * 256 + level * 16
            inner[base : base + 16, :] = block[:, lt * 128 : lt * 128 + 128]
    lane = lax.broadcasted_iota(jnp.int32, (16, 128), 1)

    def emit(load):
        carry = None
        for q in range(24):
            base, shift = (q * 500) // 128, (q * 500) % 128
            tiles = [load(q, lt) for lt in range(4)]
            if shift:
                tiles = [pltpu.roll(t, shift, 1) for t in tiles]
                low = lane < shift
                last = jnp.where(low, tiles[3], 0.0)
                tiles = [
                    jnp.where(low, carry if j == 0 else tiles[j - 1], tiles[j]) for j in range(4)
                ] + [last]
            end = (shift + 500) // 128
            for j in range(end):
                at = (base + j) * 128
                out[0, :, at : at + 128] = tiles[j][0:NLEV].astype(BF16)
            carry = tiles[end]
        out[0, :, 11904:12000] = carry[0:NLEV, 0:96].astype(BF16)

    def from_border(position):
        return lambda lt: border[pl.ds(lt * 16 * NPOS + position, 16, stride=NPOS), :]

    def from_inner(position):
        return lambda lt: inner[pl.ds(lt * 256 + position, 16, stride=16), :]

    @pl.when(row < 3)
    def _():
        emit(lambda q, lt: from_border(row * 24 + q)(lt))

    side = 72 + (row - 3) * 8

    @pl.when((row >= 3) & (row < 9))
    def _():
        emit(lambda q, lt: from_border(side + q)(lt) if q < 8 else from_inner(q - 8)(lt))

    @pl.when(row >= 9)
    def _():
        emit(lambda q, lt: from_inner(q)(lt) if q < 16 else from_border(side + q - 16)(lt))


def fields_layout(f0, f1):
    return pl.pallas_call(
        fields_kernel,
        grid=(12,),
        out_shape=jax.ShapeDtypeStruct((12, NLEV, 12000), BF16),
        in_specs=[
            pl.BlockSpec((NLEV, 1, 16, 512), lambda row: (0, jnp.maximum(row - 3, 0), 0, 0)),
            pl.BlockSpec((NLEV, NPOS, 512), lambda row: (0, 0, 0)),
        ],
        out_specs=pl.BlockSpec((1, NLEV, 12000), lambda row: (row, 0, 0)),
        scratch_shapes=[
            pltpu.VMEM((4 * 256, 128), F32),
            pltpu.VMEM((4 * 16 * NPOS, 128), F32),
        ],
        compiler_params=params(),
        cost_estimate=pl.CostEstimate(flops=0, bytes_accessed=30_000_000, transcendentals=0),
        name="fields_layout",
    )(f0.reshape(NLEV, 9, 16, 512), f1)


def moved(value, lat_steps, lon_steps):
    rows, cols = lax.axis_size("lat"), lax.axis_size("lon")
    if lon_steps == 0:
        pairs = [(i, (i + lat_steps) % rows) for i in range(rows)]
        return lax.ppermute(value, "lat", pairs)
    if lat_steps == 0:
        pairs = [(i, (i + lon_steps) % cols) for i in range(cols)]
        return lax.ppermute(value, "lon", pairs)
    pairs = []
    for i in range(rows):
        for j in range(cols):
            target = ((i + lat_steps) % rows) * cols + (j + lon_steps) % cols
            pairs.append((i * cols + j, target))
    return lax.ppermute(value, ("lat", "lon"), pairs)


def local(
    latent, skip, lat_valid, level_group, w_qkv, w_attn_out, gain_attn, w_up, w_down, gain_mlp,
    dec_query, w_dec_k, w_dec_v, w_head, w_patch, enc_embed, lat_query, w_enc_k, w_enc_v, w_enc_out,
):
    tokens = latent[0]
    in_a = moved(tokens[:, 0:3], -1, 0)
    in_b0 = moved(tokens[:, 3:9, 0:8], 0, -1)
    in_b1 = moved(tokens[:, 9:12, 16:24], 0, 1)
    in_c = moved(tokens[:, 0:3, 16:24], -1, 1)
    wq, wpv, wps, csb, ce, bias = prep(
        lat_valid, level_group, dec_query, w_dec_k, w_patch, w_enc_k, w_enc_v, lat_query, enc_embed
    )
    att, out_a, out_b0, out_b1, out_c = attend(
        tokens, in_a, in_b0, in_b1, in_c, bias, w_qkv, w_attn_out, gain_attn[None]
    )
    halos = (
        moved(out_a, 1, 0),
        moved(out_b0, 0, 1),
        moved(out_b1, 0, -1),
        moved(out_c, 1, -1),
    )
    weights = (
        w_up, w_down, gain_mlp[None], w_dec_v, wq, w_head.T, wps, wpv, csb, ce, w_enc_out,
    )
    f0, n0 = rest(0, level_group, att, (), skip[0], *weights)
    pairs = [(0, 1), (1, 0)]
    n0 = lax.ppermute(n0, "section", pairs)
    f1, n1 = rest(1, level_group, att, halos, skip[0], *weights)
    n1 = lax.ppermute(n1, "section", pairs)
    fields = fields_layout(f0.reshape(NLEV, NPOS, 512), f1.reshape(NLEV, NPOS, 512))
    fields = jnp.transpose(fields, (1, 0, 2))
    inner = n0.reshape(4, 9, 16, 512)
    top = n1[:, 0:72].reshape(4, 3, 24, 512)
    left = n1[:, 72:120].reshape(4, 6, 8, 512)
    right = n1[:, 120:144].reshape(4, 3, 8, 512)
    upper = jnp.concatenate([left, inner[:, 0:6]], axis=2)
    lower = jnp.concatenate([inner[:, 6:9], right], axis=2)
    next_latent = jnp.concatenate([top, upper, lower], axis=1)
    return (fields[None], next_latent[None])


def solution(mesh):
    return jax.shard_map(
        local,
        mesh=mesh,
        in_specs=(P("section", None, "lat", "lon", None),) * 2 + (P(),) * 18,
        out_specs=(P("section", None, "lat", "lon"), P("section", None, "lat", "lon", None)),
        check_vma=False,
    )
```

```python
import functools

import jax
import jax.numpy as jnp
import numpy as np
from jax import lax
from jax.experimental import pallas as pl
from jax.experimental.pallas import tpu as pltpu
from jax.sharding import PartitionSpec as P

F32 = jnp.float32
BF16 = jnp.bfloat16
SCALE = 0.125
MASKED = -1e30
VMEM_LIMIT = 56 * 1024 * 1024
NPOS = 144
NTOK = 4 * NPOS
NLEV = 13


def dot(a, b):
    return lax.dot_general(a, b, (((1,), (0,)), ((), ())), preferred_element_type=F32)


def dot_t(a, b):
    return lax.dot_general(a, b, (((1,), (1,)), ((), ())), preferred_element_type=F32)


def params():
    return pltpu.CompilerParams(vmem_limit_bytes=VMEM_LIMIT)


VSPEC = pl.BlockSpec(memory_space=pltpu.VMEM)
HSPEC = pl.BlockSpec(memory_space=pltpu.HBM)
SSPEC = pl.BlockSpec(memory_space=pltpu.SMEM)


def norm(value, gain):
    mean = jnp.mean(value, axis=-1, keepdims=True)
    centred = value - mean
    variance = jnp.mean(centred * centred, axis=-1, keepdims=True)
    return centred * lax.rsqrt(variance + 1e-05) * gain


def window_mask(valid, bias_out):
    lat = lax.axis_index("lat")
    masks = []
    for axis in range(2):
        token = lax.broadcasted_iota(jnp.int32, (144, 144), axis)
        masks.append((token, (token >= 72).astype(jnp.int32)))
    lines = [((t - 72 * vv) * 10923) >> 17 for t, vv in masks]
    same_level = masks[0][1] == masks[1][1]
    same_token = masks[0][0] == masks[1][0]
    for band in range(2):
        first = [(lat * 12 + 3 + band * 6 + rr) % 96 for rr in range(6)]
        labels = [sum(jnp.where(line == rr, (first[rr] + 3) // 6, 0) for rr in range(6)) for line in lines]
        real = sum(jnp.where(lines[1] == rr, valid[first[rr]], 0) for rr in range(6))
        allow = (labels[0] == labels[1]) & ((real > 0) | same_token)
        bias_out[band] = jnp.where(allow, 0.0, MASKED)
        bias_out[2 + band] = jnp.where(allow & same_level, 0.0, MASKED)


def fold(group, dq, wdk, wp, wek, wev, lq, emb, wq_out, wpv_out, wps_out, csb_out, ce_out, qb, qe):
    head16 = lax.broadcasted_iota(jnp.int32, (16, 1024), 0)
    lane16 = lax.broadcasted_iota(jnp.int32, (16, 1024), 1)
    mask16 = (lane16 >= head16 * 64) & (lane16 < head16 * 64 + 64)
    for level in range(16):
        if level < NLEV:
            row = dq[level : level + 1, :].astype(F32)
            block = jnp.where(mask16, jnp.broadcast_to(row, (16, 1024)), 0.0)
        else:
            block = jnp.zeros((16, 1024), F32)
        qb[level * 16 : level * 16 + 16, :] = block.astype(BF16)
    wq_out[...] = (dot_t(wdk[...], qb[...]) * SCALE).astype(BF16)
    head8 = lax.broadcasted_iota(jnp.int32, (8, 512), 0)
    lane8 = lax.broadcasted_iota(jnp.int32, (8, 512), 1)
    mask8 = (lane8 >= head8 * 64) & (lane8 < head8 * 64 + 64)
    qe[...] = jnp.zeros_like(qe)
    for g in range(4):
        row = lq[g : g + 1, :].astype(F32)
        qe[g * 8 : g * 8 + 8, :] = jnp.where(mask8, jnp.broadcast_to(row, (8, 512)), 0.0)
    wkq = (dot_t(wek[...], qe[...].astype(BF16)) * SCALE).astype(BF16)
    wps_out[496:512, :] = jnp.zeros((16, 128), BF16)
    wpv_out[496:512, :] = jnp.zeros((16, 512), BF16)
    wps_out[0:500, :] = dot(wp[...], wkq).astype(BF16)
    wpv_out[0:500, :] = dot(wp[...], wev[...]).astype(BF16)
    level = lax.broadcasted_iota(jnp.int32, (NLEV, 128), 0)
    lane = lax.broadcasted_iota(jnp.int32, (NLEV, 128), 1)
    mine = sum(jnp.where(level == i, group[i], 0) for i in range(NLEV))
    member = jnp.where((lane < 32) & ((lane >> 3) != mine), MASKED, 0.0)
    csb_out[0:NLEV, :] = dot(emb[...], wkq) + member
    ce_out[0:NLEV, :] = dot(emb[...], wev[...])


def inner_kernel(valid, group, gain_attn, gain_mlp, perm, perm_t, dq, lq, emb, *refs):
    far, refs = refs[0:13], refs[13:]
    (csb_out, ce_out, n_out, f_out, att_out), folded_far, backs = refs[0:5], refs[5:8], refs[8:12]
    near, folded, refs = refs[12:25], refs[25:28], refs[28:]
    lat, wqkv, wo, wdk, wp, wek, wev, wup, wdown, skip, wv, whead, wout = near
    sent, got, gone, refs = refs[0:4], refs[4:8], refs[8:12], refs[12:]
    (out, bias, x_s, xp_s, qkv_s, mix_s, qb, qe, sems, save_sems, send, recv) = refs[0:12]
    scratch = refs[12:]
    row, col = lax.axis_index("lat"), lax.axis_index("lon")
    up, down = (row + 7) % 8, (row + 1) % 8
    left, right = (col + 7) % 8, (col + 1) % 8
    barrier = greet(
        [
            {"lat": up}, {"lat": down}, {"lon": left}, {"lon": right},
            {"lat": up, "lon": right}, {"lat": down, "lon": left},
        ]
    )
    loads = [pltpu.make_async_copy(a, b, sems.at[i]) for i, (a, b) in enumerate(zip(far, near))]
    for load in loads:
        load.start()
    saves = [
        pltpu.make_async_copy(a, b, save_sems.at[i])
        for i, (a, b) in enumerate(zip(folded + (out,), folded_far + (att_out,)))
    ]
    loads[0].wait()
    for level in range(4):
        top = lat[level, 0:3].astype(F32)
        sent[0][level * 72 : level * 72 + 72, :] = top.reshape(72, 512).astype(BF16)
        sent[3][level * 24 : level * 24 + 24, :] = top[:, 16:24].reshape(24, 512).astype(BF16)
        mid = lat[level, 3:9].astype(F32)
        sent[1][level * 48 : level * 48 + 48, :] = mid[:, 0:8].reshape(48, 512).astype(BF16)
        low = lat[level, 9:12].astype(F32)
        sent[2][level * 24 : level * 24 + 24, :] = low[:, 16:24].reshape(24, 512).astype(BF16)
    pl.semaphore_wait(barrier, 6)
    targets = ({"lat": up}, {"lon": left}, {"lon": right}, {"lat": up, "lon": right})
    outward = [remote(sent[i], got[i], send, recv, i, targets[i]) for i in range(4)]
    for i in (1, 2, 3, 0):
        outward[i].start()
    window_mask(valid, bias)
    for load in loads[3:7]:
        load.wait()
    fold(group, dq, wdk, wp, wek, wev, lq, emb, *folded, csb_out, ce_out, qb, qe)
    for save in saves[0:3]:
        save.start()
    for copy in outward:
        copy.wait()
    in_a, in_b0, in_b1, in_c = got
    col8 = lax.broadcasted_iota(jnp.int32, (6, 8, 512), 1)
    for half in range(2):
        for band in range(2):
            for vv in range(2):
                level = (2 * half + vv + 1) % 4
                if band == 0:
                    own = lat[level, 3:9].astype(F32)
                    halo = in_b0[level * 48 : level * 48 + 48, :].astype(F32).reshape(6, 8, 512)
                    first = jnp.where(col8 < 6, halo, own[:, 0:8])
                    tokens = jnp.concatenate([first, own[:, 8:24]], axis=1)
                else:
                    below = in_a[level * 72 : level * 72 + 72, :].astype(F32).reshape(3, 24, 512)
                    own = jnp.concatenate([lat[level, 9:12].astype(F32), below], axis=0)
                    rows = slice(level * 24, level * 24 + 24)
                    halo = jnp.concatenate(
                        [in_b1[rows, :].astype(F32), in_c[rows, :].astype(F32)], axis=0
                    ).reshape(6, 8, 512)
                    last = jnp.where(col8 >= 2, halo, own[:, 16:24])
                    tokens = jnp.concatenate([own[:, 0:16], last], axis=1)
                base = ((half * 2 + band) * 2 + vv) * 144
                x_s[base : base + 144, :] = tokens.reshape(144, 512).astype(BF16)
            base = (half * 2 + band) * 288
            rows = slice(base, base + 288)
            xp_s[rows, :] = dot(perm[...], x_s[rows, :]).astype(BF16)

    loads[1].wait()
    for part in range(4):
        rows = slice(part * 288, part * 288 + 288)
        qkv_s[rows, :] = dot(xp_s[rows, :], wqkv[...]).astype(BF16)
    loads[2].wait()
    ones = jnp.ones((144, 128), BF16)
    lane = lax.broadcasted_iota(jnp.int32, (144, 128), 1)

    def window(block, win):
        base = block * 288 + win * 144
        rows = slice(base, base + 144)
        mask = bias[block]
        mask = jnp.concatenate([mask, mask], axis=0)
        for off in range(0, 512, 128):
            q = qkv_s[rows, off : off + 128].astype(F32) * (SCALE * 1.4426950408889634)
            k = qkv_s[rows, off + 512 : off + 640]
            v = jnp.concatenate([qkv_s[rows, off + 1024 : off + 1152], ones], axis=1)
            both = jnp.concatenate([jnp.where(lane < 64, q, 0.0), jnp.where(lane < 64, 0.0, q)], axis=0)
            s = dot_t(both.astype(BF16), k) + mask
            e = jnp.exp2(s - jnp.max(s, axis=-1, keepdims=True))
            r = dot(e.astype(BF16), v)
            r = r[:, 0:128] / r[:, 128:256]
            mix_s[rows, off : off + 128] = jnp.where(lane < 64, r[0:144], r[144:288]).astype(BF16)

    for block in range(4):
        for win in range(2):
            window(block, win)

    for half in range(2):
        for band in range(2):
            base = (half * 2 + band) * 288
            rows = slice(base, base + 288)
            back = dot(perm_t[...], mix_s[rows, :]).astype(BF16)
            o = dot(back, wo[...])
            res = x_s[rows, :].astype(F32) + norm(o, gain_attn[...])
            res = res.reshape(2, 6, 24, 512)
            for vv in range(2):
                level = half * 2 + vv
                rows = slice(level * 24, level * 24 + 24)
                if band == 0:
                    out[level, 3:9] = res[vv].astype(BF16)
                    side = res[vv, :, 0:8].reshape(48, 512)
                    gone[1][level * 48 : level * 48 + 48, :] = side.astype(BF16)
                else:
                    out[level, 9:12] = res[vv, 0:3].astype(BF16)
                    out[level, 0:3] = res[vv, 3:6].astype(BF16)
                    below = res[vv, 3:6].reshape(72, 512)
                    gone[0][level * 72 : level * 72 + 72, :] = below.astype(BF16)
                    gone[2][rows, :] = res[vv, 0:3, 16:24].reshape(24, 512).astype(BF16)
                    gone[3][rows, :] = res[vv, 3:6, 16:24].reshape(24, 512).astype(BF16)
    targets = ({"lat": down}, {"lon": right}, {"lon": left}, {"lat": down, "lon": left})
    back = [remote(gone[i], backs[i], send, recv, 4 + i, targets[i]) for i in range(4)]
    for copy in back:
        copy.start()
    saves[3].start()
    near = (wup, wdown, skip, wv, folded[0], whead, folded[2], folded[1], wout)
    order = (7, 8, 9, 10, None, 11, None, None, 12)

    def wait(i):
        if order[i] is not None:
            loads[order[i]].wait()

    cells_body(
        0, lambda level: set_tokens(0, out, level), group, gain_mlp, csb_out, ce_out, near, wait,
        f_out, n_out, scratch,
    )
    for save in saves:
        save.wait()
    for copy in back:
        copy.wait()


def window_order():
    order = []
    for cols in (list(range(6, 18)), list(range(18, 24)) + list(range(6))):
        order += [line * 24 + col for line in range(12) for col in cols]
    return np.eye(288, dtype=np.float32)[order]


def inner(valid, group, gain_attn, gain_mlp, dq, lq, emb, *far):
    sds = jax.ShapeDtypeStruct
    perm = jnp.asarray(window_order(), BF16)
    folded = [(1024, 256), (512, 512), (512, 128)]
    strips = [(288, 512), (192, 512), (96, 512), (96, 512)]
    return pl.pallas_call(
        inner_kernel,
        out_shape=(
            sds((16, 128), F32),
            sds((16, 512), F32),
            sds((4, NPOS, 512), BF16),
            sds((NLEV * NPOS, 512), BF16),
            sds((4, 12, 24, 512), BF16),
        )
        + tuple(sds(shape, BF16) for shape in folded + strips),
        in_specs=[SSPEC] * 2 + [VSPEC] * 7 + [HSPEC] * len(far),
        out_specs=(VSPEC,) * 3 + (HSPEC,) * 9,
        scratch_shapes=[pltpu.VMEM(a.shape, a.dtype) for a in far]
        + [pltpu.VMEM(shape, BF16) for shape in folded + strips * 3]
        + [
            pltpu.VMEM((4, 12, 24, 512), BF16),
            pltpu.VMEM((4, 144, 144), F32),
            pltpu.VMEM((1152, 512), BF16),
            pltpu.VMEM((1152, 512), BF16),
            pltpu.VMEM((1152, 1536), BF16),
            pltpu.VMEM((1152, 512), BF16),
            pltpu.VMEM((256, 1024), BF16),
            pltpu.VMEM((128, 512), F32),
            pltpu.SemaphoreType.DMA((13,)),
            pltpu.SemaphoreType.DMA((4,)),
            pltpu.SemaphoreType.DMA((8,)),
            pltpu.SemaphoreType.DMA((8,)),
        ]
        + cells_scratch(),
        compiler_params=pltpu.CompilerParams(
            collective_id=0, has_side_effects=True, vmem_limit_bytes=VMEM_LIMIT
        ),
        cost_estimate=pl.CostEstimate(
            flops=20_000_000_000, bytes_accessed=20_000_000, transcendentals=5_000_000
        ),
        name="attention_cells_inner",
    )(valid, group, gain_attn, gain_mlp, perm, perm.T, dq, lq, emb, *far)


def set_tokens(which, ref, level):
    own = ref[level].astype(F32)
    if which == 0:
        return jnp.concatenate([own[3:9, 8:24], own[9:12, 0:16]], axis=0).reshape(NPOS, 512)
    return jnp.concatenate(
        [
            own[0:3].reshape(72, 512),
            own[3:9, 0:8].reshape(48, 512),
            own[9:12, 16:24].reshape(24, 512),
        ],
        axis=0,
    )


def cells_body(which, tokens_of, group, gain, csb, ce, near, wait, f_out, n_out, scratch):
    (j_s, x_s, h_s, v_s, w_s, big_s, m_s, s_s, ve_s, we_s, acc_s, f_s, out_sems) = scratch
    (wup, wdown, skip, wv, wq, whead, wps, wpv, wout) = near
    for level in range(4):
        rows = slice(level * NPOS, level * NPOS + NPOS)
        x_s[rows, :] = tokens_of(level).astype(BF16)

    row = lax.broadcasted_iota(jnp.int32, (448, 1024), 0)
    head = lax.broadcasted_iota(jnp.int32, (448, 1024), 1) // 64
    big_s[...] = jnp.where(row == head + 192, 1.0, 0.0).astype(BF16)

    wait(0)

    def up(step, carry):
        cols = pl.ds(pl.multiple_of(step * 512, 512), 512)
        weight = wup[:, cols]
        for part in range(2):
            rows = slice(part * 288, part * 288 + 288)
            u = dot(x_s[rows, :], weight)
            h_s[rows, cols] = (0.5 * u * (1.0 + lax.erf(u * 0.7071067811865476))).astype(BF16)
        return carry

    lax.fori_loop(0, 4, up, 0, unroll=True)

    wait(1)

    def down(step, carry):
        rows = pl.ds(pl.multiple_of(step * 288, 288), 288)
        d = dot(h_s[rows, :], wdown[...])
        res = x_s[rows, :].astype(F32) + norm(d, gain[...])
        j_s[rows, 0:512] = res.astype(BF16)
        return carry

    lax.fori_loop(0, 2, down, 0, unroll=True)

    wait(2)
    for level in range(4):
        rows = slice(level * NPOS, level * NPOS + NPOS)
        j_s[rows, 512:1024] = set_tokens(which, skip, (level + 1) % 4).astype(BF16)
    wait(3)

    def values(step, carry):
        cols = pl.ds(pl.multiple_of(step * 256, 256), 256)
        weight = wv[:, cols]
        v0 = dot(j_s[0:NPOS, :], weight)
        v_s[0:NPOS, cols] = v0
        for level in range(1, 4):
            rows = slice(level * NPOS, level * NPOS + NPOS)
            v_s[rows, cols] = dot(j_s[rows, :], weight) - v0
        return carry

    lax.fori_loop(0, 4, values, 0, unroll=True)
    wait(4)
    scores = [dot(j_s[g * NPOS : g * NPOS + NPOS, :], wq[...]) for g in range(4)]
    top = jnp.maximum(jnp.maximum(scores[0], scores[1]), jnp.maximum(scores[2], scores[3]))
    exps = [jnp.exp(s - top) for s in scores]
    inv = 1.0 / (exps[0] + exps[1] + exps[2] + exps[3])
    for g in range(1, 4):
        w_s[(g - 1) * NPOS : g * NPOS, :] = (exps[g] * inv).astype(BF16)

    def mix(level, carry):
        spread = pl.ds(pl.multiple_of(192 - 16 * level, 16), 256)
        rows = pl.ds(pl.multiple_of(level * NPOS, NPOS), NPOS)
        for part in range(4):
            cols = slice(part * 256, part * 256 + 256)
            ex = dot(w_s[...], big_s[spread, cols])
            total = v_s[0:NPOS, cols]
            for g in range(1, 4):
                here = slice(g * NPOS, g * NPOS + NPOS)
                total = total + ex[(g - 1) * NPOS : g * NPOS] * v_s[here, cols]
            m_s[rows, cols] = total.astype(BF16)
        return carry

    lax.fori_loop(0, NLEV, mix, 0, unroll=True)

    for i in range(5, 9):
        wait(i)

    def save(step):
        rows = pl.ds(pl.multiple_of(step * 624, 624), 624)
        return pltpu.make_async_copy(f_s.at[rows], f_out.at[rows], out_sems.at[step])

    f_s[:, 384:512] = jnp.zeros((NLEV * NPOS, 128), BF16)

    def heads(step, carry):
        rows = pl.ds(pl.multiple_of(step * 624, 624), 624)
        f_s[rows, 0:500] = dot_t(m_s[rows, :], whead[...]).astype(BF16)
        f = f_s[rows, :]
        save(step).start()
        s_s[rows, :] = dot(f, wps[...])
        ve_s[rows, :] = dot(f, wpv[...])
        return carry

    [heads(i,0) for i in range(3)]

    def lev(ref, level):
        return ref[level * NPOS : level * NPOS + NPOS, :]

    top = None
    for level in range(NLEV):
        s = lev(s_s, level) + csb[level : level + 1, :]
        top = s if top is None else jnp.maximum(top, s)
    total = None
    for level in range(NLEV):
        e = jnp.exp(lev(s_s, level) + csb[level : level + 1, :] - top)
        s_s[level * NPOS : level * NPOS + NPOS, :] = e
        total = e if total is None else total + e
    inv = 1.0 / total
    for level in range(NLEV):
        we_s[level * NPOS : level * NPOS + NPOS, :] = (lev(s_s, level) * inv).astype(BF16)
    erow = lax.broadcasted_iota(jnp.int32, (128, 512), 0)
    ehead = lax.broadcasted_iota(jnp.int32, (128, 512), 1) // 64
    spread = jnp.where((erow < 32) & (erow % 8 == ehead), 1.0, 0.0).astype(BF16)
    owns = [
        [jnp.where(group[level] == g, 1.0, 0.0) for g in range(4)] for level in range(NLEV)
    ]
    for part in range(4):
        cols = slice(part * 128, part * 128 + 128)
        accs = [jnp.zeros((NPOS, 128), F32) for _ in range(4)]
        for level in range(NLEV):
            rows = slice(level * NPOS, level * NPOS + NPOS)
            ex = dot(we_s[rows, :], spread[:, cols])
            term = ex * (ve_s[rows, cols] + ce[level : level + 1, cols])
            accs = [acc + term * owns[level][g] for g, acc in enumerate(accs)]
        for g in range(4):
            acc_s[g, :, cols] = accs[g].astype(BF16)
    for g in range(4):
        n_out[g] = dot(acc_s[g], wout[...]).astype(BF16)
    for step in range(3):
        save(step).wait()


def cells_scratch():
    return [
        pltpu.VMEM((NTOK, 1024), BF16),
        pltpu.VMEM((NTOK, 512), BF16),
        pltpu.VMEM((NTOK, 2048), BF16),
        pltpu.VMEM((NTOK, 1024), F32),
        pltpu.VMEM((3 * NPOS, 256), BF16),
        pltpu.VMEM((448, 1024), BF16),
        pltpu.VMEM((NLEV * NPOS, 1024), BF16),
        pltpu.VMEM((NLEV * NPOS, 128), F32),
        pltpu.VMEM((NLEV * NPOS, 512), F32),
        pltpu.VMEM((NLEV * NPOS, 128), BF16),
        pltpu.VMEM((4, NPOS, 512), BF16),
        pltpu.VMEM((NLEV * NPOS, 512), BF16),
        pltpu.SemaphoreType.DMA((3,)),
    ]


def remote(src, dst, send, recv, i, target):
    return pltpu.make_async_remote_copy(
        src_ref=src, dst_ref=dst, send_sem=send.at[i], recv_sem=recv.at[i],
        device_id=target, device_id_type=pl.DeviceIdType.MESH,
    )


def greet(devices):
    barrier = pltpu.get_barrier_semaphore()
    for device in devices:
        pl.semaphore_signal(
            barrier, inc=1, device_id=device, device_id_type=pl.DeviceIdType.MESH
        )
    return barrier


def border_kernel(group, gain, csb, ce, n0, *refs):
    far, (f_out, n_out, n0_out), near = refs[0:14], refs[14:17], refs[17:31]
    scratch, (sems, send, recv) = refs[31:44], refs[44:]
    partner = {"section": 1 - lax.axis_index("section")}
    barrier = greet([partner])
    loads = [pltpu.make_async_copy(a, b, sems.at[i]) for i, (a, b) in enumerate(zip(far, near))]
    for load in loads:
        load.start()
    for load in loads[0:5]:
        load.wait()
    att, in_a, in_b0, in_b1, in_c = near[0:5]
    col8 = lax.broadcasted_iota(jnp.int32, (3, 8, 512), 1)

    def tokens_of(level):
        a = in_a[level].astype(F32)
        a_last = jnp.where(col8 >= 2, in_c[level].astype(F32), a[:, 16:24])
        top = jnp.concatenate([a[:, 0:16], a_last], axis=1).reshape(72, 512)
        left = jnp.where(
            jnp.concatenate([col8, col8], axis=0) < 6,
            in_b0[level].astype(F32),
            att[level, 3:9].astype(F32)[:, 0:8],
        ).reshape(48, 512)
        right = jnp.where(
            col8 >= 2, in_b1[level].astype(F32), att[level, 9:12].astype(F32)[:, 16:24]
        ).reshape(24, 512)
        return jnp.concatenate([top, left, right], axis=0)

    pl.semaphore_wait(barrier, 1)
    swap = remote(n0, n0_out, send, recv, 0, partner)
    swap.start()
    cells_body(
        1, tokens_of, group, gain, csb, ce, near[5:], lambda i: loads[5 + i].wait(), f_out, n_out,
        scratch,
    )
    swap.wait()


def border(group, gain, csb, ce, n0, *far):
    sds = jax.ShapeDtypeStruct
    return pl.pallas_call(
        border_kernel,
        out_shape=(
            sds((NLEV * NPOS, 512), BF16), sds((4, NPOS, 512), BF16), sds((4, NPOS, 512), BF16),
        ),
        in_specs=[SSPEC] + [VSPEC] * 3 + [HSPEC] * (1 + len(far)),
        out_specs=(HSPEC, VSPEC, HSPEC),
        scratch_shapes=[pltpu.VMEM(a.shape, a.dtype) for a in far]
        + cells_scratch()
        + [
            pltpu.SemaphoreType.DMA((len(far),)),
            pltpu.SemaphoreType.DMA((1,)),
            pltpu.SemaphoreType.DMA((1,)),
        ],
        compiler_params=pltpu.CompilerParams(
            collective_id=1, has_side_effects=True, vmem_limit_bytes=VMEM_LIMIT
        ),
        cost_estimate=pl.CostEstimate(
            flops=12_000_000_000, bytes_accessed=16_000_000, transcendentals=2_000_000
        ),
        name="cells_border",
    )(group, gain, csb, ce, n0, *far)


def fields_kernel(f0, f1, out, inner, border):
    row = pl.program_id(0)

    @pl.when(row == 0)
    def _():
        for level in range(NLEV):
            block = f1[level].astype(F32)
            for lt in range(4):
                base = lt * 16 * NPOS + level * NPOS
                border[base : base + NPOS, :] = block[:, lt * 128 : lt * 128 + 128]

    for level in range(NLEV):
        block = f0[level, 0].astype(F32)
        for lt in range(4):
            base = lt * 256 + level * 16
            inner[base : base + 16, :] = block[:, lt * 128 : lt * 128 + 128]
    lane = lax.broadcasted_iota(jnp.int32, (16, 128), 1)

    def emit(load):
        carry = None
        for q in range(24):
            base, shift = (q * 500) // 128, (q * 500) % 128
            tiles = [load(q, lt) for lt in range(4)]
            if shift:
                tiles = [pltpu.roll(t, shift, 1) for t in tiles]
                low = lane < shift
                last = jnp.where(low, tiles[3], 0.0)
                tiles = [
                    jnp.where(low, carry if j == 0 else tiles[j - 1], tiles[j]) for j in range(4)
                ] + [last]
            end = (shift + 500) // 128
            for j in range(end):
                at = (base + j) * 128
                out[0, :, at : at + 128] = tiles[j][0:NLEV].astype(BF16)
            carry = tiles[end]
        out[0, :, 11904:12000] = carry[0:NLEV, 0:96].astype(BF16)

    def from_border(position):
        return lambda lt: border[pl.ds(lt * 16 * NPOS + position, 16, stride=NPOS), :]

    def from_inner(position):
        return lambda lt: inner[pl.ds(lt * 256 + position, 16, stride=16), :]

    @pl.when(row < 3)
    def _():
        emit(lambda q, lt: from_border(row * 24 + q)(lt))

    side = 72 + (row - 3) * 8

    @pl.when((row >= 3) & (row < 9))
    def _():
        emit(lambda q, lt: from_border(side + q)(lt) if q < 8 else from_inner(q - 8)(lt))

    @pl.when(row >= 9)
    def _():
        emit(lambda q, lt: from_inner(q)(lt) if q < 16 else from_border(side + q - 16)(lt))


def fields_layout(f0, f1):
    return pl.pallas_call(
        fields_kernel,
        grid=(12,),
        out_shape=jax.ShapeDtypeStruct((12, NLEV, 12000), BF16),
        in_specs=[
            pl.BlockSpec((NLEV, 1, 16, 512), lambda row: (0, jnp.maximum(row - 3, 0), 0, 0)),
            pl.BlockSpec((NLEV, NPOS, 512), lambda row: (0, 0, 0)),
        ],
        out_specs=pl.BlockSpec((1, NLEV, 12000), lambda row: (row, 0, 0)),
        scratch_shapes=[
            pltpu.VMEM((4 * 256, 128), F32),
            pltpu.VMEM((4 * 16 * NPOS, 128), F32),
        ],
        compiler_params=params(),
        cost_estimate=pl.CostEstimate(flops=0, bytes_accessed=30_000_000, transcendentals=0),
        name="fields_layout",
    )(f0.reshape(NLEV, 9, 16, 512), f1)


def local(
    latent, skip, lat_valid, level_group, w_qkv, w_attn_out, gain_attn, w_up, w_down, gain_mlp,
    dec_query, w_dec_k, w_dec_v, w_head, w_patch, enc_embed, lat_query, w_enc_k, w_enc_v, w_enc_out,
):
    csb, ce, n0, f0, att, wq, wpv, wps, back_a, back_b0, back_b1, back_c = inner(
        lat_valid, level_group, gain_attn[None], gain_mlp[None], dec_query, lat_query, enc_embed,
        latent[0], w_qkv, w_attn_out, w_dec_k, w_patch, w_enc_k, w_enc_v,
        w_up, w_down, skip[0], w_dec_v, w_head.T, w_enc_out,
    )
    f1, n1, n0 = border(
        level_group, gain_mlp[None], csb, ce, n0,
        att, back_a.reshape(4, 3, 24, 512), back_b0.reshape(4, 6, 8, 512),
        back_b1.reshape(4, 3, 8, 512), back_c.reshape(4, 3, 8, 512),
        w_up, w_down, skip[0], w_dec_v, wq, w_head.T, wps, wpv, w_enc_out,
    )
    n1 = lax.ppermute(n1, "section", [(0, 1), (1, 0)])
    fields = fields_layout(f0.reshape(NLEV, NPOS, 512), f1.reshape(NLEV, NPOS, 512))
    fields = jnp.transpose(fields, (1, 0, 2))
    centre = n0.reshape(4, 9, 16, 512)
    top = n1[:, 0:72].reshape(4, 3, 24, 512)
    left = n1[:, 72:120].reshape(4, 6, 8, 512)
    right = n1[:, 120:144].reshape(4, 3, 8, 512)
    upper = jnp.concatenate([left, centre[:, 0:6]], axis=2)
    lower = jnp.concatenate([centre[:, 6:9], right], axis=2)
    next_latent = jnp.concatenate([top, upper, lower], axis=1)
    return (fields[None], next_latent[None])


def solution(mesh):
    return jax.shard_map(
        local,
        mesh=mesh,
        in_specs=(P("section", None, "lat", "lon", None),) * 2 + (P(),) * 18,
        out_specs=(P("section", None, "lat", "lon"), P("section", None, "lat", "lon", None)),
        check_vma=False,
    )
```

```python
import functools

import jax
import jax.numpy as jnp
import numpy as np
from jax import lax
from jax.experimental import pallas as pl
from jax.experimental.pallas import tpu as pltpu
from jax.sharding import PartitionSpec as P

F32 = jnp.float32
BF16 = jnp.bfloat16
SCALE = 0.125
MASKED = -1e30
VMEM_LIMIT = 60 * 1024 * 1024
NPOS = 144
NTOK = 4 * NPOS
NLEV = 13
CHUNKS = ((0, 80), (80, 64))


def dot(a, b):
    return lax.dot_general(a, b, (((1,), (0,)), ((), ())), preferred_element_type=F32)


def dot_t(a, b):
    return lax.dot_general(a, b, (((1,), (1,)), ((), ())), preferred_element_type=F32)


def params():
    return pltpu.CompilerParams(vmem_limit_bytes=VMEM_LIMIT)


VSPEC = pl.BlockSpec(memory_space=pltpu.VMEM)
HSPEC = pl.BlockSpec(memory_space=pltpu.HBM)
SSPEC = pl.BlockSpec(memory_space=pltpu.SMEM)


def norm(value, gain):
    mean = jnp.mean(value, axis=-1, keepdims=True)
    centred = value - mean
    variance = jnp.mean(centred * centred, axis=-1, keepdims=True)
    return centred * lax.rsqrt(variance + 1e-05) * gain


def window_mask(valid, bias_out):
    lat = lax.axis_index("lat")
    masks = []
    for axis in range(2):
        token = lax.broadcasted_iota(jnp.int32, (144, 144), axis)
        masks.append((token, (token >= 72).astype(jnp.int32)))
    lines = [((t - 72 * vv) * 10923) >> 17 for t, vv in masks]
    same_level = masks[0][1] == masks[1][1]
    same_token = masks[0][0] == masks[1][0]
    for band in range(2):
        first = [(lat * 12 + 3 + band * 6 + rr) % 96 for rr in range(6)]
        labels = [sum(jnp.where(line == rr, (first[rr] + 3) // 6, 0) for rr in range(6)) for line in lines]
        real = sum(jnp.where(lines[1] == rr, valid[first[rr]], 0) for rr in range(6))
        allow = (labels[0] == labels[1]) & ((real > 0) | same_token)
        bias_out[band] = jnp.where(allow, 0.0, MASKED)
        bias_out[2 + band] = jnp.where(allow & same_level, 0.0, MASKED)


def fold(group, dq, wdk, wp, wek, wev, lq, emb, wq_out, wpv_out, wps_out, csb_out, ce_out, qb, qe):
    head16 = lax.broadcasted_iota(jnp.int32, (16, 1024), 0)
    lane16 = lax.broadcasted_iota(jnp.int32, (16, 1024), 1)
    mask16 = (lane16 >= head16 * 64) & (lane16 < head16 * 64 + 64)
    for level in range(16):
        if level < NLEV:
            row = dq[level : level + 1, :].astype(F32)
            block = jnp.where(mask16, jnp.broadcast_to(row, (16, 1024)), 0.0)
        else:
            block = jnp.zeros((16, 1024), F32)
        qb[level * 16 : level * 16 + 16, :] = block.astype(BF16)
    wq_out[...] = (dot_t(wdk[...], qb[...]) * SCALE).astype(BF16)
    head8 = lax.broadcasted_iota(jnp.int32, (8, 512), 0)
    lane8 = lax.broadcasted_iota(jnp.int32, (8, 512), 1)
    mask8 = (lane8 >= head8 * 64) & (lane8 < head8 * 64 + 64)
    qe[...] = jnp.zeros_like(qe)
    for g in range(4):
        row = lq[g : g + 1, :].astype(F32)
        qe[g * 8 : g * 8 + 8, :] = jnp.where(mask8, jnp.broadcast_to(row, (8, 512)), 0.0)
    wkq = (dot_t(wek[...], qe[...].astype(BF16)) * SCALE).astype(BF16)
    wps_out[496:512, :] = jnp.zeros((16, 128), BF16)
    wpv_out[496:512, :] = jnp.zeros((16, 512), BF16)
    wps_out[0:500, :] = dot(wp[...], wkq).astype(BF16)
    wpv_out[0:500, :] = dot(wp[...], wev[...]).astype(BF16)
    level = lax.broadcasted_iota(jnp.int32, (NLEV, 128), 0)
    lane = lax.broadcasted_iota(jnp.int32, (NLEV, 128), 1)
    mine = sum(jnp.where(level == i, group[i], 0) for i in range(NLEV))
    member = jnp.where((lane < 32) & ((lane >> 3) != mine), MASKED, 0.0)
    csb_out[0:NLEV, :] = dot(emb[...], wkq) + member
    ce_out[0:NLEV, :] = dot(emb[...], wev[...])


def inner_kernel(valid, group, gain_attn, gain_mlp, perm, perm_t, dq, lq, emb, *refs):
    far, refs = refs[0:13], refs[13:]
    n_last, n_in, f_out, refs = refs[0], refs[1:3], refs[3:7], refs[7:]
    near, folded, refs = refs[0:13], refs[13:16], refs[16:]
    lat, wqkv, wo, wdk, wp, wek, wev, wup, wdown, skip, wv, whead, wout = near
    sent, got, gone, backs, refs = refs[0:4], refs[4:8], refs[8:12], refs[12:16], refs[16:]
    f_buf, n_buf, refs = refs[0:4], refs[4:7], refs[7:]
    (out, bias, csb, ce, x_s, xp_s, qkv_s, mix_s, qb, qe, sems, save_sems, send, recv) = refs[0:14]
    scratch = refs[14:]
    partner = {"section": 1 - lax.axis_index("section")}
    row, col = lax.axis_index("lat"), lax.axis_index("lon")
    up, down = (row + 7) % 8, (row + 1) % 8
    left, right = (col + 7) % 8, (col + 1) % 8
    barrier = greet(
        [
            {"lat": up}, {"lat": down}, {"lon": left}, {"lon": right},
            {"lat": up, "lon": right}, {"lat": down, "lon": left}, partner,
        ]
    )
    loads = [pltpu.make_async_copy(a, b, sems.at[i]) for i, (a, b) in enumerate(zip(far, near))]
    loads[0].start()
    saves = [pltpu.make_async_copy(f_buf[i], f_out[i], save_sems.at[i]) for i in range(4)]
    loads[0].wait()
    for level in range(4):
        top = lat[level, 0:3].astype(F32)
        sent[0][level * 72 : level * 72 + 72, :] = top.reshape(72, 512).astype(BF16)
        sent[3][level * 24 : level * 24 + 24, :] = top[:, 16:24].reshape(24, 512).astype(BF16)
        mid = lat[level, 3:9].astype(F32)
        sent[1][level * 48 : level * 48 + 48, :] = mid[:, 0:8].reshape(48, 512).astype(BF16)
        low = lat[level, 9:12].astype(F32)
        sent[2][level * 24 : level * 24 + 24, :] = low[:, 16:24].reshape(24, 512).astype(BF16)
    pl.semaphore_wait(barrier, 7)
    targets = ({"lat": up}, {"lon": left}, {"lon": right}, {"lat": up, "lon": right})
    outward = [remote(sent[i], got[i], send, recv, i, targets[i]) for i in range(4)]
    for i in (1, 2, 3, 0):
        outward[i].start()
    for load in loads[1:7]:
        load.start()
    window_mask(valid, bias)
    in_a, in_b0, in_b1, in_c = got
    col8 = lax.broadcasted_iota(jnp.int32, (6, 8, 512), 1)

    def assemble(half, band, arrived):
        for vv in range(2):
            level = (2 * half + vv + 1) % 4
            if band == 0:
                tokens = lat[level, 3:9].astype(F32)
                if arrived:
                    rows = slice(level * 48, level * 48 + 48)
                    strip = in_b0[rows, :].astype(F32).reshape(6, 8, 512)
                    first = jnp.where(col8 < 6, strip, tokens[:, 0:8])
                    tokens = jnp.concatenate([first, tokens[:, 8:24]], axis=1)
            else:
                below = in_a[level * 72 : level * 72 + 72, :].astype(F32).reshape(3, 24, 512)
                own = jnp.concatenate([lat[level, 9:12].astype(F32), below], axis=0)
                rows = slice(level * 24, level * 24 + 24)
                strip = jnp.concatenate(
                    [in_b1[rows, :].astype(F32), in_c[rows, :].astype(F32)], axis=0
                ).reshape(6, 8, 512)
                last = jnp.where(col8 >= 2, strip, own[:, 16:24])
                tokens = jnp.concatenate([own[:, 0:16], last], axis=1)
            at = ((half * 2 + band) * 2 + vv) * 144
            x_s[at : at + 144, :] = tokens.reshape(144, 512).astype(BF16)

    def reorder(half, band, first, last):
        base = (half * 2 + band) * 288
        block = x_s[base : base + 288, :]
        xp_s[base + first : base + last, :] = dot(perm[first:last, :], block).astype(BF16)

    ones = jnp.ones((144, 128), BF16)
    lane = lax.broadcasted_iota(jnp.int32, (144, 128), 1)

    def window(block, win):
        base = block * 288 + win * 144
        rows = slice(base, base + 144)
        mask = bias[block]
        mask = jnp.concatenate([mask, mask], axis=0)
        for off in range(0, 512, 128):
            q = qkv_s[rows, off : off + 128].astype(F32) * (SCALE * 1.4426950408889634)
            k = qkv_s[rows, off + 512 : off + 640]
            v = jnp.concatenate([qkv_s[rows, off + 1024 : off + 1152], ones], axis=1)
            both = jnp.concatenate([jnp.where(lane < 64, q, 0.0), jnp.where(lane < 64, 0.0, q)], axis=0)
            s = dot_t(both.astype(BF16), k) + mask
            e = jnp.exp2(s - jnp.max(s, axis=-1, keepdims=True))
            r = dot(e.astype(BF16), v)
            r = r[:, 0:128] / r[:, 128:256]
            mix_s[rows, off : off + 128] = jnp.where(lane < 64, r[0:144], r[144:288]).astype(BF16)

    for half in range(2):
        assemble(half, 0, False)
        reorder(half, 0, 0, 144)
    loads[1].wait()
    for half in range(2):
        rows = slice(half * 576, half * 576 + 144)
        qkv_s[rows, :] = dot(xp_s[rows, :], wqkv[...]).astype(BF16)
    for half in range(2):
        window(half * 2, 0)
    for load in loads[2:7]:
        load.wait()
    fold(group, dq, wdk, wp, wek, wev, lq, emb, *folded, csb, ce, qb, qe)
    for copy in outward:
        copy.wait()
    for load in loads[7:]:
        load.start()
    for half in range(2):
        assemble(half, 0, True)
        assemble(half, 1, True)
        reorder(half, 0, 144, 288)
        reorder(half, 1, 0, 288)
        rows = slice(half * 576 + 144, half * 576 + 576)
        qkv_s[rows, :] = dot(xp_s[rows, :], wqkv[...]).astype(BF16)
    for half in range(2):
        window(half * 2, 1)
        window(half * 2 + 1, 0)
        window(half * 2 + 1, 1)

    for half in range(2):
        for band in range(2):
            base = (half * 2 + band) * 288
            rows = slice(base, base + 288)
            back = dot(perm_t[...], mix_s[rows, :]).astype(BF16)
            o = dot(back, wo[...])
            res = x_s[rows, :].astype(F32) + norm(o, gain_attn[...])
            res = res.reshape(2, 6, 24, 512)
            for vv in range(2):
                level = half * 2 + vv
                rows = slice(level * 24, level * 24 + 24)
                if band == 0:
                    out[level, 3:9] = res[vv].astype(BF16)
                    side = res[vv, :, 0:8].reshape(48, 512)
                    gone[1][level * 48 : level * 48 + 48, :] = side.astype(BF16)
                else:
                    out[level, 9:12] = res[vv, 0:3].astype(BF16)
                    out[level, 0:3] = res[vv, 3:6].astype(BF16)
                    below = res[vv, 3:6].reshape(72, 512)
                    gone[0][level * 72 : level * 72 + 72, :] = below.astype(BF16)
                    gone[2][rows, :] = res[vv, 0:3, 16:24].reshape(24, 512).astype(BF16)
                    gone[3][rows, :] = res[vv, 3:6, 16:24].reshape(24, 512).astype(BF16)
    targets = ({"lat": down}, {"lon": right}, {"lon": left}, {"lat": down, "lon": left})
    back = [remote(gone[i], backs[i], send, recv, 4 + i, targets[i]) for i in range(4)]
    for copy in back:
        copy.start()
    near = (wup, wdown, skip, wv, folded[0], whead, folded[2], folded[1], wout)
    order = (7, 8, 9, 10, None, 11, None, None, 12)

    def wait(i):
        if order[i] is not None:
            loads[order[i]].wait()

    swaps = []

    def done(index):
        saves[index].start()
        if index < 3:
            off, count = CHUNKS[index % 2]
            target = n_in[index // 2].at[:, off : off + count]
            swap = remote(n_buf[index], target, send, recv, 8 + index, partner)
            swap.start()
            swaps.append(swap)

    cells_body(
        0, lambda level: set_tokens(0, out, level), group, gain_mlp, csb, ce, near, wait, scratch,
        f_buf[0:2], n_buf[0:2], done,
    )
    for copy in back:
        copy.wait()
    back_a, back_b0, back_b1, back_c = backs
    col8 = lax.broadcasted_iota(jnp.int32, (3, 8, 512), 1)

    def border_tokens(level):
        a = back_a[level * 72 : level * 72 + 72, :].astype(F32).reshape(3, 24, 512)
        b0 = back_b0[level * 48 : level * 48 + 48, :].astype(F32).reshape(6, 8, 512)
        rows = slice(level * 24, level * 24 + 24)
        b1 = back_b1[rows, :].astype(F32).reshape(3, 8, 512)
        c = back_c[rows, :].astype(F32).reshape(3, 8, 512)
        a_last = jnp.where(col8 >= 2, c, a[:, 16:24])
        top = jnp.concatenate([a[:, 0:16], a_last], axis=1).reshape(72, 512)
        both = jnp.concatenate([col8, col8], axis=0)
        left = jnp.where(both < 6, b0, out[level, 3:9].astype(F32)[:, 0:8]).reshape(48, 512)
        right = jnp.where(col8 >= 2, b1, out[level, 9:12].astype(F32)[:, 16:24]).reshape(24, 512)
        return jnp.concatenate([top, left, right], axis=0)

    cells_body(
        1, border_tokens, group, gain_mlp, csb, ce, near, lambda i: None, scratch,
        f_buf[2:4], (n_buf[2], n_last), lambda chunk: done(2 + chunk),
    )
    for save in saves:
        save.wait()
    for swap in swaps:
        swap.wait()


def window_order():
    order = []
    for cols in (list(range(6, 18)), list(range(18, 24)) + list(range(6))):
        order += [line * 24 + col for line in range(12) for col in cols]
    return np.eye(288, dtype=np.float32)[order]


def levels_to_cells(valid, group, gain_attn, gain_mlp, dq, lq, emb, *far):
    sds = jax.ShapeDtypeStruct
    perm = jnp.asarray(window_order(), BF16)
    folded = [(1024, 256), (512, 512), (512, 128)]
    strips = [(288, 512), (192, 512), (96, 512), (96, 512)]
    fields = [(NLEV * count, 512) for _, count in CHUNKS] * 2
    coded = [(4, count, 512) for _, count in CHUNKS] * 2
    return pl.pallas_call(
        inner_kernel,
        out_shape=(sds(coded[3], BF16), sds((4, NPOS, 512), BF16), sds(coded[2], BF16))
        + tuple(sds(shape, BF16) for shape in fields),
        in_specs=[SSPEC] * 2 + [VSPEC] * 7 + [HSPEC] * len(far),
        out_specs=(VSPEC,) + (HSPEC,) * 6,
        scratch_shapes=[pltpu.VMEM(a.shape, a.dtype) for a in far]
        + [pltpu.VMEM(shape, BF16) for shape in folded + strips * 4 + fields + coded[0:3]]
        + [
            pltpu.VMEM((4, 12, 24, 512), BF16),
            pltpu.VMEM((4, 144, 144), F32),
            pltpu.VMEM((16, 128), F32),
            pltpu.VMEM((16, 512), F32),
            pltpu.VMEM((1152, 512), BF16),
            pltpu.VMEM((1152, 512), BF16),
            pltpu.VMEM((1152, 1536), BF16),
            pltpu.VMEM((1152, 512), BF16),
            pltpu.VMEM((256, 1024), BF16),
            pltpu.VMEM((128, 512), F32),
            pltpu.SemaphoreType.DMA((13,)),
            pltpu.SemaphoreType.DMA((4,)),
            pltpu.SemaphoreType.DMA((11,)),
            pltpu.SemaphoreType.DMA((11,)),
        ]
        + cells_scratch(),
        compiler_params=pltpu.CompilerParams(
            collective_id=0, has_side_effects=True, vmem_limit_bytes=VMEM_LIMIT
        ),
        cost_estimate=pl.CostEstimate(
            flops=30_000_000_000, bytes_accessed=25_000_000, transcendentals=5_000_000
        ),
        name="attention_cells",
    )(valid, group, gain_attn, gain_mlp, perm, perm.T, dq, lq, emb, *far)


def set_tokens(which, ref, level):
    own = ref[level].astype(F32)
    if which == 0:
        return jnp.concatenate([own[3:9, 8:24], own[9:12, 0:16]], axis=0).reshape(NPOS, 512)
    return jnp.concatenate(
        [
            own[0:3].reshape(72, 512),
            own[3:9, 0:8].reshape(48, 512),
            own[9:12, 16:24].reshape(24, 512),
        ],
        axis=0,
    )


def cells_body(which, tokens_of, group, gain, csb, ce, near, wait, scratch, f_bufs, n_bufs, done):
    (j_s, x_s, h_s, v_s, w_s, big_s, m_s, s_s, ve_s, we_s, acc_s) = scratch
    (wup, wdown, skip, wv, wq, whead, wps, wpv, wout) = near
    for level in range(4):
        rows = slice(level * NPOS, level * NPOS + NPOS)
        x_s[rows, :] = tokens_of(level).astype(BF16)

    row = lax.broadcasted_iota(jnp.int32, (448, 1024), 0)
    head = lax.broadcasted_iota(jnp.int32, (448, 1024), 1) // 64
    if which == 0:
        big_s[...] = jnp.where(row == head + 192, 1.0, 0.0).astype(BF16)

    wait(0)

    def up(step, carry):
        cols = pl.ds(pl.multiple_of(step * 512, 512), 512)
        weight = wup[:, cols]
        for part in range(2):
            rows = slice(part * 288, part * 288 + 288)
            u = dot(x_s[rows, :], weight)
            h_s[rows, cols] = (0.5 * u * (1.0 + lax.erf(u * 0.7071067811865476))).astype(BF16)
        return carry

    lax.fori_loop(0, 4, up, 0, unroll=True)

    wait(1)

    def down(step, carry):
        rows = pl.ds(pl.multiple_of(step * 288, 288), 288)
        d = dot(h_s[rows, :], wdown[...])
        res = x_s[rows, :].astype(F32) + norm(d, gain[...])
        j_s[rows, 0:512] = res.astype(BF16)
        return carry

    lax.fori_loop(0, 2, down, 0, unroll=True)

    wait(2)
    for level in range(4):
        rows = slice(level * NPOS, level * NPOS + NPOS)
        j_s[rows, 512:1024] = set_tokens(which, skip, (level + 1) % 4).astype(BF16)
    wait(3)

    def values(step, carry):
        cols = pl.ds(pl.multiple_of(step * 256, 256), 256)
        weight = wv[:, cols]
        v0 = dot(j_s[0:NPOS, :], weight)
        v_s[0:NPOS, cols] = v0
        for level in range(1, 4):
            rows = slice(level * NPOS, level * NPOS + NPOS)
            v_s[rows, cols] = dot(j_s[rows, :], weight) - v0
        return carry

    lax.fori_loop(0, 4, values, 0, unroll=True)
    wait(4)
    scores = [dot(j_s[g * NPOS : g * NPOS + NPOS, :], wq[...]) for g in range(4)]
    top = jnp.maximum(jnp.maximum(scores[0], scores[1]), jnp.maximum(scores[2], scores[3]))
    exps = [jnp.exp(s - top) for s in scores]
    inv = 1.0 / (exps[0] + exps[1] + exps[2] + exps[3])
    for g in range(1, 4):
        w_s[(g - 1) * NPOS : g * NPOS, :] = (exps[g] * inv).astype(BF16)
    for i in range(5, 9):
        wait(i)
    owns = [
        [jnp.where(group[level] == g, 1.0, 0.0) for g in range(4)] for level in range(NLEV)
    ]
    erow = lax.broadcasted_iota(jnp.int32, (128, 512), 0)
    ehead = lax.broadcasted_iota(jnp.int32, (128, 512), 1) // 64
    spread = jnp.where((erow < 32) & (erow % 8 == ehead), 1.0, 0.0).astype(BF16)
    for chunk, (off, count) in enumerate(CHUNKS):
        part_of_set(
            off, count, owns, spread, csb, ce, near, scratch, f_bufs[chunk], n_bufs[chunk]
        )
        done(chunk)


def part_of_set(off, count, owns, spread, csb, ce, near, scratch, f_s, n_s):
    (j_s, x_s, h_s, v_s, w_s, big_s, m_s, s_s, ve_s, we_s, acc_s) = scratch
    (wup, wdown, skip, wv, wq, whead, wps, wpv, wout) = near
    weights = jnp.concatenate(
        [w_s[g * NPOS + off : g * NPOS + off + count, :] for g in range(3)], axis=0
    )

    def lev(level):
        return slice(level * count, level * count + count)

    for level in range(NLEV):
        spread_rows = slice(192 - 16 * level, 448 - 16 * level)
        for part in range(4):
            cols = slice(part * 256, part * 256 + 256)
            ex = dot(weights, big_s[spread_rows, cols])
            total = v_s[off : off + count, cols]
            for g in range(1, 4):
                here = slice(g * NPOS + off, g * NPOS + off + count)
                total = total + ex[(g - 1) * count : g * count] * v_s[here, cols]
            m_s[lev(level), cols] = total.astype(BF16)
    whole = slice(0, NLEV * count)
    f_s[whole, 384:512] = jnp.zeros((NLEV * count, 128), BF16)
    for rows in (slice(0, 7 * count), slice(7 * count, NLEV * count)):
        f_s[rows, 0:500] = dot_t(m_s[rows, :], whead[...]).astype(BF16)
        f = f_s[rows, :]
        s_s[rows, :] = dot(f, wps[...])
        ve_s[rows, :] = dot(f, wpv[...])
    top = None
    for level in range(NLEV):
        s = s_s[lev(level), :] + csb[level : level + 1, :]
        top = s if top is None else jnp.maximum(top, s)
    total = None
    for level in range(NLEV):
        e = jnp.exp(s_s[lev(level), :] + csb[level : level + 1, :] - top)
        s_s[lev(level), :] = e
        total = e if total is None else total + e
    inv = 1.0 / total
    for level in range(NLEV):
        we_s[lev(level), :] = (s_s[lev(level), :] * inv).astype(BF16)
    for first, last in ((0, 7), (7, NLEV)):
        ex = dot(we_s[first * count : last * count, :], spread)
        for level in range(first, last):
            mine = ex[(level - first) * count : (level - first + 1) * count]
            ve_s[lev(level), :] = mine * (ve_s[lev(level), :] + ce[level : level + 1, :])
    for part in range(4):
        cols = slice(part * 128, part * 128 + 128)
        accs = [jnp.zeros((count, 128), F32) for _ in range(4)]
        for level in range(NLEV):
            term = ve_s[lev(level), cols]
            accs = [acc + term * owns[level][g] for g, acc in enumerate(accs)]
        for g in range(4):
            acc_s[g, 0:count, cols] = accs[g].astype(BF16)
    for g in range(4):
        n_s[g] = dot(acc_s[g, 0:count, :], wout[...]).astype(BF16)


def cells_scratch():
    most = NLEV * CHUNKS[0][1]
    return [
        pltpu.VMEM((NTOK, 1024), BF16),
        pltpu.VMEM((NTOK, 512), BF16),
        pltpu.VMEM((NTOK, 2048), BF16),
        pltpu.VMEM((NTOK, 1024), F32),
        pltpu.VMEM((3 * NPOS, 256), BF16),
        pltpu.VMEM((448, 1024), BF16),
        pltpu.VMEM((most, 1024), BF16),
        pltpu.VMEM((most, 128), F32),
        pltpu.VMEM((most, 512), F32),
        pltpu.VMEM((most, 128), BF16),
        pltpu.VMEM((4, CHUNKS[0][1], 512), BF16),
    ]


def remote(src, dst, send, recv, i, target):
    return pltpu.make_async_remote_copy(
        src_ref=src, dst_ref=dst, send_sem=send.at[i], recv_sem=recv.at[i],
        device_id=target, device_id_type=pl.DeviceIdType.MESH,
    )


def greet(devices):
    barrier = pltpu.get_barrier_semaphore()
    for device in devices:
        pl.semaphore_signal(
            barrier, inc=1, device_id=device, device_id_type=pl.DeviceIdType.MESH
        )
    return barrier


def fields_kernel(*refs):
    far, out_far, next_far, near = refs[0:6], refs[6], refs[7], refs[8:14]
    inner, border, out, coded, sems, out_sems = refs[14:]
    loads = [pltpu.make_async_copy(far[i], near[i], sems.at[i]) for i in range(6)]
    for i in (2, 3, 0, 1, 4, 5):
        loads[i].start()

    def spread(store, which):
        for chunk, (off, count) in enumerate(CHUNKS):
            loads[2 * which + chunk].wait()
            for level in range(NLEV):
                block = near[2 * which + chunk][level * count : level * count + count, :]
                block = block.astype(F32)
                for lt in range(4):
                    base = lt * 16 * NPOS + level * NPOS + off
                    store[base : base + count, :] = block[:, lt * 128 : lt * 128 + 128]

    lane = lax.broadcasted_iota(jnp.int32, (16, 128), 1)

    def at(store, position):
        return [store[pl.ds(lt * 16 * NPOS + position, 16, stride=NPOS), :] for lt in range(4)]

    def save(row):
        return pltpu.make_async_copy(out.at[row], out_far.at[row], out_sems.at[row])

    def emit(row, load):
        carry = None
        for q in range(24):
            base, shift = (q * 500) // 128, (q * 500) % 128
            tiles = load(q)
            if shift:
                tiles = [pltpu.roll(t, shift, 1) for t in tiles]
                low = lane < shift
                last = jnp.where(low, tiles[3], 0.0)
                tiles = [
                    jnp.where(low, carry if j == 0 else tiles[j - 1], tiles[j]) for j in range(4)
                ] + [last]
            end = (shift + 500) // 128
            for j in range(end):
                cols = slice((base + j) * 128, (base + j) * 128 + 128)
                out[row, :, cols] = tiles[j][0:NLEV].astype(BF16)
            carry = tiles[end]
        out[row, :, 11904:12000] = carry[0:NLEV, 0:96].astype(BF16)
        save(row).start()

    def top(row, carry):
        emit(row, lambda q: at(border, row * 24 + q))
        return carry

    def middle(row, carry):
        side = 72 + (row - 3) * 8
        here = (row - 3) * 16
        emit(row, lambda q: at(border, side + q) if q < 8 else at(inner, here + q - 8))
        return carry

    def bottom(row, carry):
        side = 72 + (row - 3) * 8
        here = (row - 3) * 16
        emit(row, lambda q: at(inner, here + q) if q < 16 else at(border, side + q - 16))
        return carry

    spread(border, 1)
    lax.fori_loop(0, 3, top, 0)
    spread(inner, 0)
    lax.fori_loop(3, 9, middle, 0)
    lax.fori_loop(9, 12, bottom, 0)
    loads[4].wait()
    loads[5].wait()
    blank = jnp.zeros((5, 8, 512), F32)
    for level in range(4):
        centre = near[4][level].astype(F32).reshape(9, 16, 512)
        edge = near[5][level].astype(F32)
        left = jnp.concatenate([edge[72:80].reshape(1, 8, 512), blank], axis=0)
        upper = jnp.concatenate([left, centre[0:6]], axis=1)
        lower = jnp.concatenate([centre[6:9], blank[0:3]], axis=1)
        coded[level, 0:3] = edge[0:72].reshape(3, 24, 512).astype(BF16)
        coded[level, 3:9] = upper.astype(BF16)
        coded[level, 9:12] = lower.astype(BF16)
    last = pltpu.make_async_copy(coded, next_far, out_sems.at[12])
    last.start()
    for row in range(12):
        save(row).wait()
    last.wait()


def fields_layout(*parts):
    return pl.pallas_call(
        fields_kernel,
        out_shape=(
            jax.ShapeDtypeStruct((12, NLEV, 12000), BF16),
            jax.ShapeDtypeStruct((4, 12, 24, 512), BF16),
        ),
        in_specs=[HSPEC] * 6,
        out_specs=(HSPEC, HSPEC),
        scratch_shapes=[pltpu.VMEM(a.shape, a.dtype) for a in parts]
        + [
            pltpu.VMEM((4 * 16 * NPOS, 128), F32),
            pltpu.VMEM((4 * 16 * NPOS, 128), F32),
            pltpu.VMEM((12, NLEV, 12000), BF16),
            pltpu.VMEM((4, 12, 24, 512), BF16),
            pltpu.SemaphoreType.DMA((6,)),
            pltpu.SemaphoreType.DMA((13,)),
        ],
        compiler_params=params(),
        cost_estimate=pl.CostEstimate(flops=0, bytes_accessed=30_000_000, transcendentals=0),
        name="fields_layout",
    )(*parts)


def local(
    latent, skip, lat_valid, level_group, w_qkv, w_attn_out, gain_attn, w_up, w_down, gain_mlp,
    dec_query, w_dec_k, w_dec_v, w_head, w_patch, enc_embed, lat_query, w_enc_k, w_enc_v, w_enc_out,
):
    n1b, n0, n1a, *parts = levels_to_cells(
        lat_valid, level_group, gain_attn[None], gain_mlp[None], dec_query, lat_query, enc_embed,
        latent[0], w_qkv, w_attn_out, w_dec_k, w_patch, w_enc_k, w_enc_v,
        w_up, w_down, skip[0], w_dec_v, w_head.T, w_enc_out,
    )
    n1b = lax.ppermute(n1b, "section", [(0, 1), (1, 0)])
    fields, known = fields_layout(*parts, n0, n1a)
    fields = jnp.transpose(fields, (1, 0, 2))
    side = jnp.pad(n1b.reshape(4, 8, 8, 512), ((0, 0), (4, 0), (0, 0), (0, 0)))
    row = jnp.arange(12, dtype=jnp.int32)[None, :, None, None]
    col = jnp.arange(24, dtype=jnp.int32)[None, None, :, None]
    late = ((row >= 4) & (row < 9) & (col < 8)) | ((row >= 9) & (col >= 16))
    next_latent = jnp.where(late, jnp.concatenate([side, side, side], axis=2), known)
    return (fields[None], next_latent[None])


def solution(mesh):
    return jax.shard_map(
        local,
        mesh=mesh,
        in_specs=(P("section", None, "lat", "lon", None),) * 2 + (P(),) * 18,
        out_specs=(P("section", None, "lat", "lon"), P("section", None, "lat", "lon", None)),
        check_vma=False,
    )
```

```python
import functools

import jax
import jax.numpy as jnp
import numpy as np
from jax import lax
from jax.experimental import pallas as pl
from jax.experimental.pallas import tpu as pltpu
from jax.sharding import PartitionSpec as P

F32 = jnp.float32
BF16 = jnp.bfloat16
SCALE = 0.125
MASKED = -1e30
VMEM_LIMIT = 60 * 1024 * 1024
NPOS = 144
NTOK = 4 * NPOS
NLEV = 13
CHUNKS = ((0, 80), (80, 64))


def dot(a, b):
    return lax.dot_general(a, b, (((1,), (0,)), ((), ())), preferred_element_type=F32)


def dot_t(a, b):
    return lax.dot_general(a, b, (((1,), (1,)), ((), ())), preferred_element_type=F32)


def params():
    return pltpu.CompilerParams(vmem_limit_bytes=VMEM_LIMIT)


VSPEC = pl.BlockSpec(memory_space=pltpu.VMEM)
HSPEC = pl.BlockSpec(memory_space=pltpu.HBM)
SSPEC = pl.BlockSpec(memory_space=pltpu.SMEM)


def norm(value, gain):
    mean = jnp.mean(value, axis=-1, keepdims=True)
    centred = value - mean
    variance = jnp.mean(centred * centred, axis=-1, keepdims=True)
    return centred * lax.rsqrt(variance + 1e-05) * gain


def window_mask(valid, bias_out):
    lat = lax.axis_index("lat")
    masks = []
    for axis in range(2):
        token = lax.broadcasted_iota(jnp.int32, (144, 144), axis)
        masks.append((token, (token >= 72).astype(jnp.int32)))
    lines = [((t - 72 * vv) * 10923) >> 17 for t, vv in masks]
    same_level = masks[0][1] == masks[1][1]
    same_token = masks[0][0] == masks[1][0]
    for band in range(2):
        first = [(lat * 12 + 3 + band * 6 + rr) % 96 for rr in range(6)]
        labels = [sum(jnp.where(line == rr, (first[rr] + 3) // 6, 0) for rr in range(6)) for line in lines]
        real = sum(jnp.where(lines[1] == rr, valid[first[rr]], 0) for rr in range(6))
        allow = (labels[0] == labels[1]) & ((real > 0) | same_token)
        bias_out[band] = jnp.where(allow, 0.0, MASKED)
        bias_out[2 + band] = jnp.where(allow & same_level, 0.0, MASKED)


def fold(group, dq, wdk, wp, wek, wev, lq, emb, wq_out, wpv_out, wps_out, csb_out, ce_out, qb, qe):
    head16 = lax.broadcasted_iota(jnp.int32, (16, 1024), 0)
    lane16 = lax.broadcasted_iota(jnp.int32, (16, 1024), 1)
    mask16 = (lane16 >= head16 * 64) & (lane16 < head16 * 64 + 64)
    for level in range(16):
        if level < NLEV:
            row = dq[level : level + 1, :].astype(F32)
            block = jnp.where(mask16, jnp.broadcast_to(row, (16, 1024)), 0.0)
        else:
            block = jnp.zeros((16, 1024), F32)
        qb[level * 16 : level * 16 + 16, :] = block.astype(BF16)
    wq_out[...] = (dot_t(wdk[...], qb[...]) * SCALE).astype(BF16)
    head8 = lax.broadcasted_iota(jnp.int32, (8, 512), 0)
    lane8 = lax.broadcasted_iota(jnp.int32, (8, 512), 1)
    mask8 = (lane8 >= head8 * 64) & (lane8 < head8 * 64 + 64)
    qe[...] = jnp.zeros_like(qe)
    for g in range(4):
        row = lq[g : g + 1, :].astype(F32)
        qe[g * 8 : g * 8 + 8, :] = jnp.where(mask8, jnp.broadcast_to(row, (8, 512)), 0.0)
    wkq = (dot_t(wek[...], qe[...].astype(BF16)) * SCALE).astype(BF16)
    wps_out[496:512, :] = jnp.zeros((16, 128), BF16)
    wpv_out[496:512, :] = jnp.zeros((16, 512), BF16)
    wps_out[0:500, :] = dot(wp[...], wkq).astype(BF16)
    wpv_out[0:500, :] = dot(wp[...], wev[...]).astype(BF16)
    level = lax.broadcasted_iota(jnp.int32, (NLEV, 128), 0)
    lane = lax.broadcasted_iota(jnp.int32, (NLEV, 128), 1)
    mine = sum(jnp.where(level == i, group[i], 0) for i in range(NLEV))
    member = jnp.where((lane < 32) & ((lane >> 3) != mine), MASKED, 0.0)
    csb_out[0:NLEV, :] = dot(emb[...], wkq) + member
    ce_out[0:NLEV, :] = dot(emb[...], wev[...])


def inner_kernel(valid, group, gain_attn, gain_mlp, perm, perm_t, dq, lq, emb, *refs):
    far, refs = refs[0:13], refs[13:]
    n_last, n_in, f_out, refs = refs[0], refs[1:3], refs[3:7], refs[7:]
    near, folded, refs = refs[0:13], refs[13:16], refs[16:]
    lat, wqkv, wo, wdk, wp, wek, wev, wup, wdown, skip, wv, whead, wout = near
    sent, got, gone, backs, refs = refs[0:4], refs[4:8], refs[8:12], refs[12:16], refs[16:]
    f_buf, n_buf, refs = refs[0:4], refs[4:7], refs[7:]
    (out, bias, csb, ce, x_s, xp_s, qkv_s, mix_s, qb, qe, sems, save_sems, send, recv) = refs[0:14]
    scratch = refs[14:]
    partner = {"section": 1 - lax.axis_index("section")}
    row, col = lax.axis_index("lat"), lax.axis_index("lon")
    up, down = (row + 7) % 8, (row + 1) % 8
    left, right = (col + 7) % 8, (col + 1) % 8
    barrier = greet(
        [
            {"lat": up}, {"lat": down}, {"lon": left}, {"lon": right},
            {"lat": up, "lon": right}, {"lat": down, "lon": left}, partner,
        ]
    )
    loads = [pltpu.make_async_copy(a, b, sems.at[i]) for i, (a, b) in enumerate(zip(far, near))]
    loads[0].start()
    saves = [pltpu.make_async_copy(f_buf[i], f_out[i], save_sems.at[i]) for i in range(4)]
    loads[0].wait()
    for level in range(4):
        top = lat[level, 0:3].astype(F32)
        sent[0][level * 72 : level * 72 + 72, :] = top.reshape(72, 512).astype(BF16)
        sent[3][level * 24 : level * 24 + 24, :] = top[:, 16:24].reshape(24, 512).astype(BF16)
        mid = lat[level, 3:9].astype(F32)
        sent[1][level * 48 : level * 48 + 48, :] = mid[:, 0:8].reshape(48, 512).astype(BF16)
        low = lat[level, 9:12].astype(F32)
        sent[2][level * 24 : level * 24 + 24, :] = low[:, 16:24].reshape(24, 512).astype(BF16)
    pl.semaphore_wait(barrier, 7)
    targets = ({"lat": up}, {"lon": left}, {"lon": right}, {"lat": up, "lon": right})
    outward = [remote(sent[i], got[i], send, recv, i, targets[i]) for i in range(4)]
    for i in (1, 2, 3, 0):
        outward[i].start()
    for load in loads[1:7]:
        load.start()
    window_mask(valid, bias)
    in_a, in_b0, in_b1, in_c = got
    col8 = lax.broadcasted_iota(jnp.int32, (6, 8, 512), 1)

    def assemble(half, band, arrived):
        for vv in range(2):
            level = (2 * half + vv + 1) % 4
            if band == 0:
                tokens = lat[level, 3:9].astype(F32)
                if arrived:
                    rows = slice(level * 48, level * 48 + 48)
                    strip = in_b0[rows, :].astype(F32).reshape(6, 8, 512)
                    first = jnp.where(col8 < 6, strip, tokens[:, 0:8])
                    tokens = jnp.concatenate([first, tokens[:, 8:24]], axis=1)
            else:
                below = in_a[level * 72 : level * 72 + 72, :].astype(F32).reshape(3, 24, 512)
                own = jnp.concatenate([lat[level, 9:12].astype(F32), below], axis=0)
                rows = slice(level * 24, level * 24 + 24)
                strip = jnp.concatenate(
                    [in_b1[rows, :].astype(F32), in_c[rows, :].astype(F32)], axis=0
                ).reshape(6, 8, 512)
                last = jnp.where(col8 >= 2, strip, own[:, 16:24])
                tokens = jnp.concatenate([own[:, 0:16], last], axis=1)
            at = ((half * 2 + band) * 2 + vv) * 144
            x_s[at : at + 144, :] = tokens.reshape(144, 512).astype(BF16)

    def reorder(half, band, first, last):
        base = (half * 2 + band) * 288
        block = x_s[base : base + 288, :]
        xp_s[base + first : base + last, :] = dot(perm[first:last, :], block).astype(BF16)

    ones = jnp.ones((144, 128), BF16)
    lane = lax.broadcasted_iota(jnp.int32, (144, 128), 1)

    def window(block, win):
        base = block * 288 + win * 144
        rows = slice(base, base + 144)
        mask = bias[block]
        mask = jnp.concatenate([mask, mask], axis=0)
        for off in range(0, 512, 128):
            q = qkv_s[rows, off : off + 128].astype(F32) * (SCALE * 1.4426950408889634)
            k = qkv_s[rows, off + 512 : off + 640]
            v = jnp.concatenate([qkv_s[rows, off + 1024 : off + 1152], ones], axis=1)
            both = jnp.concatenate([jnp.where(lane < 64, q, 0.0), jnp.where(lane < 64, 0.0, q)], axis=0)
            s = dot_t(both.astype(BF16), k) + mask
            e = jnp.exp2(s - jnp.max(s, axis=-1, keepdims=True))
            r = dot(e.astype(BF16), v)
            r = r[:, 0:128] / r[:, 128:256]
            mix_s[rows, off : off + 128] = jnp.where(lane < 64, r[0:144], r[144:288]).astype(BF16)

    for half in range(2):
        assemble(half, 0, False)
        reorder(half, 0, 0, 144)
    loads[1].wait()
    for half in range(2):
        rows = slice(half * 576, half * 576 + 144)
        qkv_s[rows, :] = dot(xp_s[rows, :], wqkv[...]).astype(BF16)
    for half in range(2):
        window(half * 2, 0)
    for load in loads[2:7]:
        load.wait()
    fold(group, dq, wdk, wp, wek, wev, lq, emb, *folded, csb, ce, qb, qe)
    for copy in outward:
        copy.wait()
    for load in loads[7:]:
        load.start()
    for half in range(2):
        assemble(half, 0, True)
        assemble(half, 1, True)
        reorder(half, 0, 144, 288)
        reorder(half, 1, 0, 288)
        rows = slice(half * 576 + 144, half * 576 + 576)
        qkv_s[rows, :] = dot(xp_s[rows, :], wqkv[...]).astype(BF16)
    for half in range(2):
        window(half * 2, 1)
        window(half * 2 + 1, 0)
        window(half * 2 + 1, 1)

    for half in range(2):
        for band in range(2):
            base = (half * 2 + band) * 288
            rows = slice(base, base + 288)
            back = dot(perm_t[...], mix_s[rows, :]).astype(BF16)
            o = dot(back, wo[...])
            res = x_s[rows, :].astype(F32) + norm(o, gain_attn[...])
            res = res.reshape(2, 6, 24, 512)
            for vv in range(2):
                level = half * 2 + vv
                rows = slice(level * 24, level * 24 + 24)
                if band == 0:
                    out[level, 3:9] = res[vv].astype(BF16)
                    side = res[vv, :, 0:8].reshape(48, 512)
                    gone[1][level * 48 : level * 48 + 48, :] = side.astype(BF16)
                else:
                    out[level, 9:12] = res[vv, 0:3].astype(BF16)
                    out[level, 0:3] = res[vv, 3:6].astype(BF16)
                    below = res[vv, 3:6].reshape(72, 512)
                    gone[0][level * 72 : level * 72 + 72, :] = below.astype(BF16)
                    gone[2][rows, :] = res[vv, 0:3, 16:24].reshape(24, 512).astype(BF16)
                    gone[3][rows, :] = res[vv, 3:6, 16:24].reshape(24, 512).astype(BF16)
    targets = ({"lat": down}, {"lon": right}, {"lon": left}, {"lat": down, "lon": left})
    back = [remote(gone[i], backs[i], send, recv, 4 + i, targets[i]) for i in range(4)]
    for copy in back:
        copy.start()
    near = (wup, wdown, skip, wv, folded[0], whead, folded[2], folded[1], wout)
    order = (7, 8, 9, 10, None, 11, None, None, 12)

    def wait(i):
        if order[i] is not None:
            loads[order[i]].wait()

    swaps = []

    def done(index):
        saves[index].start()
        if index < 3:
            off, count = CHUNKS[index % 2]
            target = n_in[index // 2].at[:, off : off + count]
            swap = remote(n_buf[index], target, send, recv, 8 + index, partner)
            swap.start()
            swaps.append(swap)

    cells_body(
        0, lambda level: set_tokens(0, out, level), group, gain_mlp, csb, ce, near, wait, scratch,
        f_buf[0:2], n_buf[0:2], done,
    )
    for copy in back:
        copy.wait()
    back_a, back_b0, back_b1, back_c = backs
    col8 = lax.broadcasted_iota(jnp.int32, (3, 8, 512), 1)

    def border_tokens(level):
        a = back_a[level * 72 : level * 72 + 72, :].astype(F32).reshape(3, 24, 512)
        b0 = back_b0[level * 48 : level * 48 + 48, :].astype(F32).reshape(6, 8, 512)
        rows = slice(level * 24, level * 24 + 24)
        b1 = back_b1[rows, :].astype(F32).reshape(3, 8, 512)
        c = back_c[rows, :].astype(F32).reshape(3, 8, 512)
        a_last = jnp.where(col8 >= 2, c, a[:, 16:24])
        top = jnp.concatenate([a[:, 0:16], a_last], axis=1).reshape(72, 512)
        both = jnp.concatenate([col8, col8], axis=0)
        left = jnp.where(both < 6, b0, out[level, 3:9].astype(F32)[:, 0:8]).reshape(48, 512)
        right = jnp.where(col8 >= 2, b1, out[level, 9:12].astype(F32)[:, 16:24]).reshape(24, 512)
        return jnp.concatenate([top, left, right], axis=0)

    cells_body(
        1, border_tokens, group, gain_mlp, csb, ce, near, lambda i: None, scratch,
        f_buf[2:4], (n_buf[2], n_last), lambda chunk: done(2 + chunk),
    )
    for save in saves:
        save.wait()
    for swap in swaps:
        swap.wait()


def window_order():
    order = []
    for cols in (list(range(6, 18)), list(range(18, 24)) + list(range(6))):
        order += [line * 24 + col for line in range(12) for col in cols]
    return np.eye(288, dtype=np.float32)[order]


def levels_to_cells(valid, group, gain_attn, gain_mlp, dq, lq, emb, *far):
    sds = jax.ShapeDtypeStruct
    perm = jnp.asarray(window_order(), BF16)
    folded = [(1024, 256), (512, 512), (512, 128)]
    strips = [(288, 512), (192, 512), (96, 512), (96, 512)]
    fields = [(NLEV * count, 512) for _, count in CHUNKS] * 2
    coded = [(4, count, 512) for _, count in CHUNKS] * 2
    return pl.pallas_call(
        inner_kernel,
        out_shape=(sds(coded[3], BF16), sds((4, NPOS, 512), BF16), sds(coded[2], BF16))
        + tuple(sds(shape, BF16) for shape in fields),
        in_specs=[SSPEC] * 2 + [VSPEC] * 7 + [HSPEC] * len(far),
        out_specs=(VSPEC,) + (HSPEC,) * 6,
        scratch_shapes=[pltpu.VMEM(a.shape, a.dtype) for a in far]
        + [pltpu.VMEM(shape, BF16) for shape in folded + strips * 4 + fields + coded[0:3]]
        + [
            pltpu.VMEM((4, 12, 24, 512), BF16),
            pltpu.VMEM((4, 144, 144), F32),
            pltpu.VMEM((16, 128), F32),
            pltpu.VMEM((16, 512), F32),
            pltpu.VMEM((1152, 512), BF16),
            pltpu.VMEM((1152, 512), BF16),
            pltpu.VMEM((1152, 1536), BF16),
            pltpu.VMEM((1152, 512), BF16),
            pltpu.VMEM((256, 1024), BF16),
            pltpu.VMEM((128, 512), F32),
            pltpu.SemaphoreType.DMA((13,)),
            pltpu.SemaphoreType.DMA((4,)),
            pltpu.SemaphoreType.DMA((11,)),
            pltpu.SemaphoreType.DMA((11,)),
        ]
        + cells_scratch(),
        compiler_params=pltpu.CompilerParams(
            collective_id=0, has_side_effects=True, vmem_limit_bytes=VMEM_LIMIT
        ),
        cost_estimate=pl.CostEstimate(
            flops=30_000_000_000, bytes_accessed=25_000_000, transcendentals=5_000_000
        ),
        name="attention_cells",
    )(valid, group, gain_attn, gain_mlp, perm, perm.T, dq, lq, emb, *far)


def set_tokens(which, ref, level):
    own = ref[level].astype(F32)
    if which == 0:
        return jnp.concatenate([own[3:9, 8:24], own[9:12, 0:16]], axis=0).reshape(NPOS, 512)
    return jnp.concatenate(
        [
            own[0:3].reshape(72, 512),
            own[3:9, 0:8].reshape(48, 512),
            own[9:12, 16:24].reshape(24, 512),
        ],
        axis=0,
    )


def cells_body(which, tokens_of, group, gain, csb, ce, near, wait, scratch, f_bufs, n_bufs, done):
    (j_s, x_s, h_s, v_s, w_s, big_s, m_s, s_s, ve_s, we_s, acc_s) = scratch
    (wup, wdown, skip, wv, wq, whead, wps, wpv, wout) = near
    for level in range(4):
        rows = slice(level * NPOS, level * NPOS + NPOS)
        x_s[rows, :] = tokens_of(level).astype(BF16)

    row = lax.broadcasted_iota(jnp.int32, (448, 1024), 0)
    head = lax.broadcasted_iota(jnp.int32, (448, 1024), 1) // 64
    if which == 0:
        big_s[...] = jnp.where(row == head + 192, 1.0, 0.0).astype(BF16)

    wait(0)

    def up(step, carry):
        cols = pl.ds(pl.multiple_of(step * 512, 512), 512)
        weight = wup[:, cols]
        for part in range(2):
            rows = slice(part * 288, part * 288 + 288)
            u = dot(x_s[rows, :], weight)
            h_s[rows, cols] = (0.5 * u * (1.0 + lax.erf(u * 0.7071067811865476))).astype(BF16)
        return carry

    lax.fori_loop(0, 4, up, 0, unroll=True)

    wait(1)

    def down(step, carry):
        rows = pl.ds(pl.multiple_of(step * 288, 288), 288)
        d = dot(h_s[rows, :], wdown[...])
        res = x_s[rows, :].astype(F32) + norm(d, gain[...])
        j_s[rows, 0:512] = res.astype(BF16)
        return carry

    lax.fori_loop(0, 2, down, 0, unroll=True)

    wait(2)
    for level in range(4):
        rows = slice(level * NPOS, level * NPOS + NPOS)
        j_s[rows, 512:1024] = set_tokens(which, skip, (level + 1) % 4).astype(BF16)
    wait(3)

    def values(step, carry):
        cols = pl.ds(pl.multiple_of(step * 256, 256), 256)
        weight = wv[:, cols]
        v0 = dot(j_s[0:NPOS, :], weight)
        v_s[0:NPOS, cols] = v0
        for level in range(1, 4):
            rows = slice(level * NPOS, level * NPOS + NPOS)
            v_s[rows, cols] = dot(j_s[rows, :], weight) - v0
        return carry

    lax.fori_loop(0, 4, values, 0, unroll=True)
    wait(4)
    scores = [dot(j_s[g * NPOS : g * NPOS + NPOS, :], wq[...]) for g in range(4)]
    top = jnp.maximum(jnp.maximum(scores[0], scores[1]), jnp.maximum(scores[2], scores[3]))
    exps = [jnp.exp(s - top) for s in scores]
    inv = 1.0 / (exps[0] + exps[1] + exps[2] + exps[3])
    for g in range(1, 4):
        w_s[(g - 1) * NPOS : g * NPOS, :] = (exps[g] * inv).astype(BF16)
    for i in range(5, 9):
        wait(i)
    owns = [
        [jnp.where(group[level] == g, 1.0, 0.0) for g in range(4)] for level in range(NLEV)
    ]
    erow = lax.broadcasted_iota(jnp.int32, (128, 512), 0)
    ehead = lax.broadcasted_iota(jnp.int32, (128, 512), 1) // 64
    spread = jnp.where((erow < 32) & (erow % 8 == ehead), 1.0, 0.0).astype(BF16)
    for chunk, (off, count) in enumerate(CHUNKS):
        part_of_set(
            off, count, owns, spread, csb, ce, near, scratch, f_bufs[chunk], n_bufs[chunk]
        )
        done(chunk)


def part_of_set(off, count, owns, spread, csb, ce, near, scratch, f_s, n_s):
    (j_s, x_s, h_s, v_s, w_s, big_s, m_s, s_s, ve_s, we_s, acc_s) = scratch
    (wup, wdown, skip, wv, wq, whead, wps, wpv, wout) = near
    weights = jnp.concatenate(
        [w_s[g * NPOS + off : g * NPOS + off + count, :] for g in range(3)], axis=0
    )

    def lev(level):
        return slice(level * count, level * count + count)

    for level in range(NLEV):
        spread_rows = slice(192 - 16 * level, 448 - 16 * level)
        for part in range(4):
            cols = slice(part * 256, part * 256 + 256)
            ex = dot(weights, big_s[spread_rows, cols])
            total = v_s[off : off + count, cols]
            for g in range(1, 4):
                here = slice(g * NPOS + off, g * NPOS + off + count)
                total = total + ex[(g - 1) * count : g * count] * v_s[here, cols]
            m_s[lev(level), cols] = total.astype(BF16)
    whole = slice(0, NLEV * count)
    f_s[whole, 384:512] = jnp.zeros((NLEV * count, 128), BF16)
    for rows in (slice(0, 7 * count), slice(7 * count, NLEV * count)):
        f_s[rows, 0:500] = dot_t(m_s[rows, :], whead[...]).astype(BF16)
        f = f_s[rows, :]
        s_s[rows, :] = dot(f, wps[...])
        ve_s[rows, :] = dot(f, wpv[...])
    top = None
    for level in range(NLEV):
        s = s_s[lev(level), :] + csb[level : level + 1, :]
        top = s if top is None else jnp.maximum(top, s)
    total = None
    for level in range(NLEV):
        e = jnp.exp(s_s[lev(level), :] + csb[level : level + 1, :] - top)
        s_s[lev(level), :] = e
        total = e if total is None else total + e
    inv = 1.0 / total
    for level in range(NLEV):
        we_s[lev(level), :] = (s_s[lev(level), :] * inv).astype(BF16)
    for first, last in ((0, 7), (7, NLEV)):
        ex = dot(we_s[first * count : last * count, :], spread)
        for level in range(first, last):
            mine = ex[(level - first) * count : (level - first + 1) * count]
            ve_s[lev(level), :] = mine * (ve_s[lev(level), :] + ce[level : level + 1, :])
    for part in range(4):
        cols = slice(part * 128, part * 128 + 128)
        accs = [jnp.zeros((count, 128), F32) for _ in range(4)]
        for level in range(NLEV):
            term = ve_s[lev(level), cols]
            accs = [acc + term * owns[level][g] for g, acc in enumerate(accs)]
        for g in range(4):
            acc_s[g, 0:count, cols] = accs[g].astype(BF16)
    for g in range(4):
        n_s[g] = dot(acc_s[g, 0:count, :], wout[...]).astype(BF16)


def cells_scratch():
    most = NLEV * CHUNKS[0][1]
    return [
        pltpu.VMEM((NTOK, 1024), BF16),
        pltpu.VMEM((NTOK, 512), BF16),
        pltpu.VMEM((NTOK, 2048), BF16),
        pltpu.VMEM((NTOK, 1024), F32),
        pltpu.VMEM((3 * NPOS, 256), BF16),
        pltpu.VMEM((448, 1024), BF16),
        pltpu.VMEM((most, 1024), BF16),
        pltpu.VMEM((most, 128), F32),
        pltpu.VMEM((most, 512), F32),
        pltpu.VMEM((most, 128), BF16),
        pltpu.VMEM((4, CHUNKS[0][1], 512), BF16),
    ]


def remote(src, dst, send, recv, i, target):
    return pltpu.make_async_remote_copy(
        src_ref=src, dst_ref=dst, send_sem=send.at[i], recv_sem=recv.at[i],
        device_id=target, device_id_type=pl.DeviceIdType.MESH,
    )


def greet(devices):
    barrier = pltpu.get_barrier_semaphore()
    for device in devices:
        pl.semaphore_signal(
            barrier, inc=1, device_id=device, device_id_type=pl.DeviceIdType.MESH
        )
    return barrier


def fields_kernel(*refs):
    far, out_far, next_far, near = refs[0:6], refs[6], refs[7], refs[8:14]
    inner, border, out, coded, sems, out_sems = refs[14:]
    loads = [pltpu.make_async_copy(far[i], near[i], sems.at[i]) for i in range(6)]
    for i in (2, 3, 0, 1, 4, 5):
        loads[i].start()

    def spread(store, which):
        for chunk, (off, count) in enumerate(CHUNKS):
            loads[2 * which + chunk].wait()
            for level in range(NLEV):
                block = near[2 * which + chunk][level * count : level * count + count, :]
                block = block.astype(F32)
                for lt in range(4):
                    base = lt * 16 * NPOS + level * NPOS + off
                    store[base : base + count, :] = block[:, lt * 128 : lt * 128 + 128]

    lane = lax.broadcasted_iota(jnp.int32, (16, 128), 1)

    def at(store, position):
        return [store[pl.ds(lt * 16 * NPOS + position, 16, stride=NPOS), :] for lt in range(4)]

    def save(row):
        return pltpu.make_async_copy(out.at[row], out_far.at[row], out_sems.at[row])

    def emit(row, load):
        carry = None
        for q in range(24):
            base, shift = (q * 500) // 128, (q * 500) % 128
            tiles = load(q)
            if shift:
                tiles = [pltpu.roll(t, shift, 1) for t in tiles]
                low = lane < shift
                last = jnp.where(low, tiles[3], 0.0)
                tiles = [
                    jnp.where(low, carry if j == 0 else tiles[j - 1], tiles[j]) for j in range(4)
                ] + [last]
            end = (shift + 500) // 128
            for j in range(end):
                cols = slice((base + j) * 128, (base + j) * 128 + 128)
                out[row, :, cols] = tiles[j][0:NLEV].astype(BF16)
            carry = tiles[end]
        out[row, :, 11904:12000] = carry[0:NLEV, 0:96].astype(BF16)
        save(row).start()

    def top(row, carry):
        emit(row, lambda q: at(border, row * 24 + q))
        return carry

    def middle(row, carry):
        side = 72 + (row - 3) * 8
        here = (row - 3) * 16
        emit(row, lambda q: at(border, side + q) if q < 8 else at(inner, here + q - 8))
        return carry

    def bottom(row, carry):
        side = 72 + (row - 3) * 8
        here = (row - 3) * 16
        emit(row, lambda q: at(inner, here + q) if q < 16 else at(border, side + q - 16))
        return carry

    spread(border, 1)
    lax.fori_loop(0, 3, top, 0)
    spread(inner, 0)
    lax.fori_loop(3, 9, middle, 0)
    lax.fori_loop(9, 12, bottom, 0)
    loads[4].wait()
    loads[5].wait()
    blank = jnp.zeros((5, 8, 512), F32)
    for level in range(4):
        centre = near[4][level].astype(F32).reshape(9, 16, 512)
        edge = near[5][level].astype(F32)
        left = jnp.concatenate([edge[72:80].reshape(1, 8, 512), blank], axis=0)
        upper = jnp.concatenate([left, centre[0:6]], axis=1)
        lower = jnp.concatenate([centre[6:9], blank[0:3]], axis=1)
        coded[level, 0:3] = edge[0:72].reshape(3, 24, 512).astype(BF16)
        coded[level, 3:9] = upper.astype(BF16)
        coded[level, 9:12] = lower.astype(BF16)
    last = pltpu.make_async_copy(coded, next_far, out_sems.at[12])
    last.start()
    for row in range(12):
        save(row).wait()
    last.wait()


def fields_layout(*parts):
    return pl.pallas_call(
        fields_kernel,
        out_shape=(
            jax.ShapeDtypeStruct((12, NLEV, 12000), BF16),
            jax.ShapeDtypeStruct((4, 12, 24, 512), BF16),
        ),
        in_specs=[HSPEC] * 6,
        out_specs=(HSPEC, HSPEC),
        scratch_shapes=[pltpu.VMEM(a.shape, a.dtype) for a in parts]
        + [
            pltpu.VMEM((4 * 16 * NPOS, 128), F32),
            pltpu.VMEM((4 * 16 * NPOS, 128), F32),
            pltpu.VMEM((12, NLEV, 12000), BF16),
            pltpu.VMEM((4, 12, 24, 512), BF16),
            pltpu.SemaphoreType.DMA((6,)),
            pltpu.SemaphoreType.DMA((13,)),
        ],
        compiler_params=params(),
        cost_estimate=pl.CostEstimate(flops=0, bytes_accessed=30_000_000, transcendentals=0),
        name="fields_layout",
    )(*parts)


def local(
    latent, skip, lat_valid, level_group, w_qkv, w_attn_out, gain_attn, w_up, w_down, gain_mlp,
    dec_query, w_dec_k, w_dec_v, w_head, w_patch, enc_embed, lat_query, w_enc_k, w_enc_v, w_enc_out,
):
    n1b, n0, n1a, *parts = levels_to_cells(
        lat_valid, level_group, gain_attn[None], gain_mlp[None], dec_query, lat_query, enc_embed,
        latent[0], w_qkv, w_attn_out, w_dec_k, w_patch, w_enc_k, w_enc_v,
        w_up, w_down, skip[0], w_dec_v, w_head.T, w_enc_out,
    )
    n1b = lax.ppermute(n1b, "section", [(0, 1), (1, 0)])
    fields, known = fields_layout(*parts, n0, n1a)
    fields = jnp.transpose(fields, (1, 0, 2))
    side = n1b.reshape(4, 8, 8, 512)
    next_latent = known.at[:, 4:9, 0:8].set(side[:, 0:5]).at[:, 9:12, 16:24].set(side[:, 5:8])
    return (fields[None], next_latent[None])


def solution(mesh):
    return jax.shard_map(
        local,
        mesh=mesh,
        in_specs=(P("section", None, "lat", "lon", None),) * 2 + (P(),) * 18,
        out_specs=(P("section", None, "lat", "lon"), P("section", None, "lat", "lon", None)),
        check_vma=False,
    )
```
